128 devices in a mesh: dp: 16 (over y, x), chan: 4 (over z_lo, core), row: 2 (over z_hi).
Axes of the slice: x: 4, y: 4, z: 4 (z_hi: 2, z_lo: 2; z = z_hi * 2 + z_lo), core: 2. Of those that a mesh axis runs over, the one named last changes fastest.
Arguments:
- images: bfloat16 [16, 128, 320, 128], P('dp', 'row', 'chan'), may hold values from -6 to 6
- kernel: bfloat16 [9, 320, 320], P(None, 'dp', 'chan'), may hold values from -0.109375 to 0.109375
- cotangent: bfloat16 [16, 128, 320, 128], P('dp', 'row', 'chan'), may hold values from -6 to 6
Outputs:
- activated: bfloat16 [16, 128, 320, 128], P('dp', 'row', 'chan')
- input_grad: float32 [16, 128, 320, 128], P('dp', 'row', 'chan')
- kernel_grad: float32 [9, 320, 320], P(None, 'dp', 'chan')
The draws below stay inside these ranges and needn't reach their ends.
All inputs are finite; a program needn't handle non-finite values.
Results may differ from the reference program's by a relative error of at most 0.0029.
Values may be sent and summed in bfloat16 or wider, within the bound.
A program may use at most 192 MiB of HBM per device.

```python
import jax
import jax.numpy as jnp

C = 320
W = 128
BATCH = 16
H = 128


def raised(drawn, rng, source, target, blocks, factor):
    def block_of(axis_at):
        return (jnp.arange(drawn.shape[axis_at]) // (drawn.shape[axis_at] // blocks)).reshape((-1,) + (1,) * (drawn.ndim - 1 - axis_at))

    first = jax.random.permutation(rng, blocks)[block_of(target)]
    other_side = (block_of(target) + blocks // 2) % blocks
    return jnp.where((block_of(source) == first) | (block_of(source) == other_side), factor * drawn, drawn)


def level_of(rng, dims, pieces, low, high):
    loudness = 1.0
    for position, blocks in pieces:
        heights = jax.random.uniform(jax.random.fold_in(jax.random.fold_in(rng, 6), position), (blocks,), jnp.float32, low / len(pieces), high / len(pieces))
        loudness = loudness * jnp.repeat(jnp.exp(heights), dims[position] // blocks).reshape((-1,) + (1,) * (len(dims) - 1 - position))
    return loudness


def bell_draw(rng, dims, spread, limit, split=(), dtype=jnp.bfloat16):
    loudness = level_of(rng, dims, split, -0.22, 0.18) if split else 1.0
    values = jax.random.normal(rng, dims, jnp.float32) * spread * loudness
    return jnp.minimum(jnp.maximum(values, -limit), limit).astype(dtype)


def noise_with(stream_key, shape, deviation, limit, shards, heavy, held_as=jnp.bfloat16):
    values = deviation * jax.random.normal(stream_key, shape, jnp.float32)
    if shards:
        values = values * level_of(stream_key, shape, shards, -0.22, 0.18)
    return jnp.clip(raised(values, jax.random.fold_in(stream_key, 3), *heavy), -limit, limit).astype(held_as)


def setup_inputs(seed: int = 0) -> dict:
    key_list = jax.random.split(jax.random.key(seed), 4)
    images = noise_with(key_list[0], (BATCH, H, C, W), 1.0, 6.0, ((0, 16), (1, 2), (2, 4)), (0, 2, 16, 2.0))
    kernel = bell_draw(key_list[1], (9, C, C), (9 * C) ** -0.5, 0.109375, ((1, 16), (2, 4)))
    cotangent = bell_draw(key_list[2], (BATCH, H, C, W), 1.0, 6.0, ((0, 16), (1, 2), (2, 4)))
    return dict(images=images, kernel=kernel, cotangent=cotangent)


def window_at(padded, tap_row, tap_col, height, width):
    return padded[:, tap_row:tap_row + height, :, tap_col:tap_col + width]


def reference(images, kernel, cotangent):
    batch_count, height, channels, width = images.shape
    padded = jnp.pad(images, ((0, 0), (1, 1), (0, 0), (1, 1)))
    kernel_wide = kernel.astype(jnp.float32)
    pre = jnp.zeros((batch_count, height, kernel.shape[2], width), jnp.float32)
    for tap_row in range(3):
        for tap_col in range(3):
            window = window_at(padded, tap_row, tap_col, height, width).astype(jnp.float32)
            pre = pre + jnp.einsum("nhiw,io->nhow", window, kernel_wide[3 * tap_row + tap_col])
    activated = jax.nn.silu(pre).astype(jnp.bfloat16)
    sigma = jax.nn.sigmoid(pre)
    slope = (cotangent.astype(jnp.float32) * sigma * (1.0 + pre * (1.0 - sigma))).astype(jnp.bfloat16)
    slope_padded = jnp.pad(slope, ((0, 0), (1, 1), (0, 0), (1, 1)))
    slope_wide = slope.astype(jnp.float32)
    input_grad = jnp.zeros((batch_count, height, channels, width), jnp.float32)
    grads = []
    for tap_row in range(3):
        for tap_col in range(3):
            window = window_at(slope_padded, 2 - tap_row, 2 - tap_col, height, width).astype(jnp.float32)
            input_grad = input_grad + jnp.einsum("nhow,io->nhiw", window, kernel_wide[3 * tap_row + tap_col])
            source = window_at(padded, tap_row, tap_col, height, width).astype(jnp.float32)
            grads.append(jnp.einsum("nhiw,nhow->io", source, slope_wide))
    return activated, input_grad, jnp.stack(grads)
```

```python
import functools
import math

import jax
import jax.numpy as jnp
from jax import lax
from jax.experimental import pallas as pl
from jax.experimental.pallas import tpu as pltpu
from jax.sharding import PartitionSpec as P

MESH = pl.DeviceIdType.MESH
BF16 = jnp.bfloat16
F32 = jnp.float32
ROWS = 4


def round_up(x, m):
    return (x + m - 1) // m * m


def remote(src, dst, send, recv, **where):
    return pltpu.make_async_remote_copy(
        src_ref=src, dst_ref=dst, send_sem=send, recv_sem=recv, device_id=where, device_id_type=MESH
    )


def shift_right(x):
    lane = lax.broadcasted_iota(jnp.int32, x.shape, 1)
    return jnp.where(lane == 0, 0.0, pltpu.roll(x, 1, 1))


def shift_left(x):
    lane = lax.broadcasted_iota(jnp.int32, x.shape, 1)
    return jnp.where(lane == x.shape[1] - 1, 0.0, pltpu.roll(x, x.shape[1] - 1, 1))


def body(
    side, own, share, height, width,
    img, ker, cot,
    act_out, in_own, in_other, kg_out,
    xs, gs, ss, s3, acc, wk, wpk, wraw, em, wf, wb, ab, pf, pb,
    kin, kp, kr, ksum, kr2, kt, kq,
    local, wsend, wrecv, isend, irecv, hsend, hrecv, bsend, brecv,
    ssend, srecv, asend, arecv, alocal, plocal, psend, precv, csend, crecv, ksend, krecv,
):
    rows = height // 2
    chunks = rows // ROWS
    chip = 2 * own
    every = 4 * own
    pad_share = wpk.shape[1]
    lanes = s3.shape[0] // 2

    dp = lax.axis_index("dp")
    chan = lax.axis_index("chan")
    row = lax.axis_index("row")
    l = chan // 2
    c = lax.rem(chan, 2)
    sib = 2 * l + 1 - c
    other = 2 * (1 - l)
    y = dp // side
    x = lax.rem(dp, side)
    first = jnp.where(c == 0, x, y)
    second = jnp.where(c == 0, y, x)
    step_first = jnp.where(c == 0, 1, side)
    step_second = jnp.where(c == 0, side, 1)

    def on_first(k):
        f = lax.rem(first + k, side)
        return f, f * step_first + second * step_second

    def on_second(k):
        s = lax.rem(second + k, side)
        return s, first * step_first + s * step_second

    barrier = pltpu.get_barrier_semaphore()
    count = 0
    for k in range(1, 4):
        pl.semaphore_signal(barrier, inc=1, device_id={"chan": lax.rem(chan + k, 4)}, device_id_type=MESH)
        count += 1
    for g in range(4):
        pl.semaphore_signal(barrier, inc=1, device_id={"row": 1 - row, "chan": g}, device_id_type=MESH)
        count += 1
    for k in range(1, side):
        pl.semaphore_signal(barrier, inc=1, device_id={"dp": on_first(k)[1]}, device_id_type=MESH)
        pl.semaphore_signal(barrier, inc=1, device_id={"dp": on_second(k)[1]}, device_id_type=MESH)
        count += 2

    def mine(ref, first_row, n, g):
        return ref.at[pl.ds(first_row, n), pl.ds(pl.multiple_of(own * g, 16), own)]

    load_k = pltpu.make_async_copy(ker, wk, local.at[0])
    load_k.start()
    load_x = pltpu.make_async_copy(
        img.at[pl.ds((rows - 1) * c, rows + 1)], mine(xs, 1 - c, rows + 1, chan), local.at[1]
    )
    load_x.start()
    load_g = pltpu.make_async_copy(cot.at[pl.ds(rows * c, rows)], mine(gs, 0, rows, c), local.at[2])
    load_g.start()

    wpk[...] = jnp.zeros_like(wpk)
    for core in range(2):
        s3[core * lanes + 3 * own : (core + 1) * lanes, :] = jnp.zeros((lanes - 3 * own, s3.shape[1]), BF16)

    @pl.when(jnp.logical_and(c == 0, row == 0))
    def _():
        xs[0] = jnp.zeros(xs.shape[1:], BF16)
        ss[0] = jnp.zeros(ss.shape[1:], BF16)

    @pl.when(jnp.logical_and(c == 1, row == 1))
    def _():
        xs[rows + 1] = jnp.zeros(xs.shape[1:], BF16)
        ss[rows + 1] = jnp.zeros(ss.shape[1:], BF16)

    acc[...] = jnp.zeros_like(acc)
    load_k.wait()
    for b in range(3):
        for a in range(3):
            wpk[b, a * share : (a + 1) * share, 0:own] = wk[3 * a + b].astype(F32)
    wraw[c, second, first] = wpk[...].astype(BF16)

    pl.semaphore_wait(barrier, count)

    gather = []
    for k in range(1, side):
        spot = wraw.at[c, second, first]
        copy = remote(spot, spot, wsend.at[0, k], wrecv.at[0, k], dp=on_first(k)[1])
        copy.start()
        gather.append(copy)

    pieces = [(rows - ROWS, ROWS + 1), (1, ROWS + 1)]
    pieces += [(ROWS * k + 2, ROWS) for k in range(1, chunks - 2)]
    pieces += [(ROWS * (chunks - 2) + 2, ROWS - 2)]
    sent = []
    for to in range(2):
        copy = remote(
            img.at[pl.ds(rows - to, 1)], mine(xs, (rows + 1) * (1 - to), 1, chan),
            isend.at[to, chunks], irecv.at[c, chunks], chan=other + to,
        )
        copy.start()
        sent.append(copy)
        copy = remote(
            img.at[pl.ds((height - 1) * (1 - row), 1)], mine(xs, (rows + 1) * row, 1, chan),
            hsend.at[to], hrecv.at[chan], row=1 - row, chan=2 * to + row,
        )
        copy.start()
        sent.append(copy)
    copy = remote(
        img.at[pl.ds((rows - 1) * (1 - c), rows + 1)], mine(xs, c, rows + 1, chan),
        bsend.at[0], brecv.at[0], chan=sib,
    )
    copy.start()
    sent.append(copy)
    for s, (start, n) in enumerate(pieces):
        for to in range(2):
            copy = remote(
                img.at[pl.ds(rows * to + start - 1, n)], mine(xs, start, n, chan),
                isend.at[to, s], irecv.at[c, s], chan=other + to,
            )
            copy.start()
            sent.append(copy)
        if s == 0:
            copy = remote(
                cot.at[pl.ds(rows * (1 - c), rows)], mine(gs, 0, rows, c), bsend.at[1], brecv.at[1], chan=sib
            )
            copy.start()
            sent.append(copy)

    spot = lax.broadcasted_iota(jnp.int32, (1, em.shape[1]), 1)
    owner = jnp.zeros_like(spot)
    for k in range(1, side * side):
        owner += (spot >= k * pad_share).astype(jnp.int32)
    within = spot - owner * pad_share
    tap = (within >= share).astype(jnp.int32) + (within >= 2 * share).astype(jnp.int32)
    target = tap * every + owner * share + within - tap * share
    target = jnp.where(within < 3 * share, target, -1)
    em[...] = (lax.broadcasted_iota(jnp.int32, em.shape, 0) == target).astype(F32).astype(BF16)

    for k in range(1, side):
        gather[k - 1].wait()
    for k in range(1, side):
        spot = wraw.at[c, second]
        copy = remote(spot, spot, wsend.at[1, k], wrecv.at[1, k], dp=on_second(k)[1])
        copy.start()
        gather.append(copy)
    for k in range(1, side):
        gather[side - 2 + k].wait()
    copy = remote(wraw.at[c], wraw.at[c], bsend.at[2], brecv.at[2], chan=sib)
    copy.start()
    sent.append(copy)
    remote(wraw.at[c], wraw.at[1 - c], bsend.at[2], brecv.at[2], chan=sib).wait_recv()

    wide = 2 * wraw.shape[-1]
    fold = (
        lax.broadcasted_iota(jnp.int32, (wide, 3 * chip), 0),
        lax.broadcasted_iota(jnp.int32, (wide, 3 * chip), 1),
    )
    half = wide // 2
    core_of = (fold[0] >= half).astype(jnp.int32)
    inside = fold[0] - core_of * half
    for b in range(3):
        blocks = []
        for core in range(2):
            order = [(i, j) if core == 0 else (j, i) for i in range(side) for j in range(side)]
            blocks.append(jnp.concatenate([wraw[core, i, j, b] for i, j in order], axis=0))
        taps = jnp.dot(em[...], jnp.concatenate(blocks, axis=1), preferred_element_type=F32)
        turned = jnp.transpose(taps).astype(BF16)
        for core in range(2):
            wf[b * chip + core * own : b * chip + (core + 1) * own, :] = turned[core * half : core * half + own]
        narrow = taps.astype(BF16)
        total = jnp.zeros((every, 3 * chip), F32)
        for a in range(3):
            goal = (2 - a) * chip + core_of * own + inside
            place = jnp.logical_and(fold[1] == goal, inside < own).astype(F32).astype(BF16)
            total += jnp.dot(narrow[a * every : (a + 1) * every], place, preferred_element_type=F32)
        total = total.astype(BF16)
        for part in range(2):
            base = pl.multiple_of(b * every + chip * jnp.where(l == part, 0, 1), 16)
            wb[pl.ds(base, chip), :] = total[part * chip : (part + 1) * chip]

    load_x.wait()
    load_g.wait()
    for which, ref in ((0, mine(xs, 1 - c, rows + 1, sib)), (1, mine(gs, 0, rows, 1 - c))):
        remote(ref, ref, bsend.at[which], brecv.at[which], chan=sib).wait_recv()
    for of in range(2):
        ref = mine(xs, (rows + 1) * (1 - c), 1, other + of)
        remote(ref, ref, isend.at[of, chunks], irecv.at[of, chunks], chan=other + of).wait_recv()

    @pl.when(c != row)
    def _():
        for g in range(4):
            ref = mine(xs, (rows + 1) * c, 1, g)
            remote(ref, ref, hsend.at[0], hrecv.at[g], row=1 - row, chan=g).wait_recv()

    def await_rows(s, start, n):
        for of in range(2):
            ref = mine(xs, start, n, other + of)
            remote(ref, ref, isend.at[of, s], irecv.at[of, s], chan=other + of).wait_recv()

    place = 2 * row + c

    def down_copy():
        return remote(ss.at[rows], ss.at[0], ssend.at[0], srecv.at[0], row=row + c, chan=sib)

    def up_copy():
        return remote(ss.at[1], ss.at[rows + 1], ssend.at[1], srecv.at[1], row=row - (1 - c), chan=sib)

    def act_copies(k):
        at = pl.ds(k * ROWS, ROWS)
        to = pl.ds(rows * c + k * ROWS, ROWS)
        return (
            pltpu.make_async_copy(ab.at[c, at], act_out.at[to], alocal.at[k]),
            remote(ab.at[1 - c, at], act_out.at[to], asend.at[k], arecv.at[k], chan=sib),
        )

    def grad_copies(k):
        at = pl.ds(k * ROWS, ROWS)
        to = pl.ds(rows * c + k * ROWS, ROWS)
        return (
            pltpu.make_async_copy(pf.at[c, at], in_own.at[to], plocal.at[k]),
            remote(pf.at[1 - c, at], in_own.at[to], psend.at[k], precv.at[k], chan=sib),
            remote(pb.at[0, at], in_other.at[to], csend.at[0, k], crecv.at[c, k], chan=other),
            remote(pb.at[1, at], in_other.at[to], csend.at[1, k], crecv.at[c, k], chan=other + 1),
        )

    def three(ref, start):
        block = ref[pl.ds(start, 3)]
        return block.reshape(3 * ref.shape[1], width)

    def forward(k):
        for pair in range(ROWS // 2):
            q = k * ROWS + 2 * pair
            right = jnp.concatenate([three(xs, q), three(xs, q + 1)], axis=1)
            taps = jnp.dot(wf[...], right, preferred_element_type=F32)
            for u in range(2):
                at = slice(u * width, (u + 1) * width)
                pre = shift_right(taps[0:chip, at]) + taps[chip : 2 * chip, at] + shift_left(taps[2 * chip :, at])
                sigma = 1.0 / (1.0 + jnp.exp(-pre))
                done = (pre * sigma).astype(BF16)
                for core in range(2):
                    ab[core, q + u] = done[core * own : (core + 1) * own]
                slope = gs[q + u].astype(F32) * sigma * (1.0 + pre * (1.0 - sigma))
                slope = slope.astype(BF16)
                ss[q + u + 1] = slope
                wide_slope = slope.astype(F32)
                turned = (shift_left(wide_slope).astype(BF16), slope, shift_right(wide_slope).astype(BF16))
                to = slice((2 * pair + u) * width, (2 * pair + u + 1) * width)
                for core in range(2):
                    for b in range(3):
                        s3[core * lanes + b * own : core * lanes + (b + 1) * own, to] = turned[b][
                            core * own : (core + 1) * own
                        ]
        left = jnp.concatenate([three(xs, k * ROWS + u) for u in range(ROWS)], axis=1)
        term = lax.dot_general(left, s3[...], (((1,), (1,)), ((), ())), preferred_element_type=F32)
        for core in range(2):
            acc[core] += term[:, core * lanes : (core + 1) * lanes]

    def backward(k):
        for pair in range(ROWS // 2):
            q = k * ROWS + 2 * pair
            right = jnp.concatenate([three(ss, q), three(ss, q + 1)], axis=1)
            taps = jnp.dot(wb[...], right, preferred_element_type=F32)
            for u in range(2):
                at = slice(u * width, (u + 1) * width)
                grad = (
                    shift_left(taps[0:every, at])
                    + taps[every : 2 * every, at]
                    + shift_right(taps[2 * every :, at])
                )
                for core in range(2):
                    pf[core, q + u] = grad[core * own : (core + 1) * own]
                    pb[core, q + u] = grad[chip + core * own : chip + (core + 1) * own].astype(BF16)

    @pl.loop(0, chunks + 3)
    def _(s):
        for fixed in (0, 1, chunks - 1):

            @pl.when(s == fixed)
            def _():
                await_rows(fixed, *pieces[fixed])

        @pl.when(jnp.logical_and(s > 1, s < chunks - 1))
        def _():
            await_rows(s, ROWS * (s - 1) + 2, ROWS)

        @pl.when(s < chunks)
        def _():
            k = lax.rem(s + chunks - 1, chunks)
            forward(k)
            for copy in act_copies(k):
                copy.start()

        @pl.when(jnp.logical_and(s == 0, place < 3))
        def _():
            down_copy().start()

        @pl.when(jnp.logical_and(s == 1, place > 0))
        def _():
            up_copy().start()

        @pl.when(jnp.logical_and(s == chunks + 1, place < 3))
        def _():
            up_copy().wait_recv()

        @pl.when(jnp.logical_and(s == chunks + 2, place > 0))
        def _():
            down_copy().wait_recv()

        @pl.when(s >= 3)
        def _():
            k = lax.rem(s - 2, chunks)
            backward(k)
            for copy in grad_copies(k):
                copy.start()

        @pl.when(s == chunks - 1)
        def _():
            remote(acc.at[1 - c], kin, ksend.at[0, 0], krecv.at[0, 0], chan=sib).start()

    trade = remote(acc.at[1 - c], kin, ksend.at[0, 0], krecv.at[0, 0], chan=sib)
    trade.wait()
    kin[...] += acc[c]
    for i in range(side):
        for j in range(side):
            f = jnp.where(c == 0, j, i)
            s = jnp.where(c == 0, i, j)
            d = i * side + j
            for a in range(3):
                kp[f, s, a * share : (a + 1) * share, :] = kin[a * every + d * share : a * every + (d + 1) * share, :]
    copies = []
    for k in range(1, side):
        f, to = on_first(k)
        copy = remote(kp.at[f], kr.at[k], ksend.at[1, k], krecv.at[1, k], dp=to)
        copy.start()
        copies.append(copy)
    for copy in copies:
        copy.wait()
    total = kp[first]
    for k in range(1, side):
        total += kr[k]
    ksum[...] = total
    copies = []
    for k in range(1, side):
        s, to = on_second(k)
        copy = remote(ksum.at[s], kr2.at[k], ksend.at[2, k], krecv.at[2, k], dp=to)
        copy.start()
        copies.append(copy)
    for copy in copies:
        copy.wait()
    total = ksum[second]
    for k in range(1, side):
        total += kr2[k]
    kt[...] = total
    copy = remote(kt, kq, ksend.at[3, 0], krecv.at[3, 0], row=1 - row)
    copy.start()
    copy.wait()
    kt[...] += kq[...]
    store = pltpu.make_async_copy(kt, kg_out, local.at[3])
    store.start()

    for copy in sent:
        copy.wait_send()

    @pl.when(place < 3)
    def _():
        down_copy().wait_send()

    @pl.when(place > 0)
    def _():
        up_copy().wait_send()

    @pl.loop(0, chunks)
    def _(k):
        keep, give = act_copies(k)
        keep.wait()
        give.wait()
        keep, give, low, high = grad_copies(k)
        keep.wait()
        give.wait()
        low.wait_send()
        high.wait_send()
        for of in range(2):
            ref = in_other.at[pl.ds(rows * of + k * ROWS, ROWS)]
            remote(ref, ref, csend.at[of, k], crecv.at[of, k], chan=other + of).wait_recv()

    store.wait()


def shards(images, kernel, cotangent):
    _, height, own, width = images.shape
    share = kernel.shape[1]
    side = math.isqrt(lax.axis_size("dp"))
    rows = height // 2
    chunks = rows // ROWS
    chip, every = 2 * own, 4 * own
    pad_share = round_up(3 * share, 16)
    pad_own = round_up(own, 128)
    lanes = round_up(3 * own, 128)
    dma = pltpu.SemaphoreType.DMA
    scratch = [
        pltpu.VMEM((rows + 2, every, width), BF16),
        pltpu.VMEM((rows, chip, width), BF16),
        pltpu.VMEM((rows + 2, chip, width), BF16),
        pltpu.VMEM((2 * lanes, ROWS * width), BF16),
        pltpu.VMEM((2, 3 * every, lanes), F32),
        pltpu.VMEM(kernel.shape, BF16),
        pltpu.VMEM((3, pad_share, pad_own), F32),
        pltpu.VMEM((2, side, side, 3, pad_share, pad_own), BF16),
        pltpu.VMEM((3 * every, side * side * pad_share), BF16),
        pltpu.VMEM((3 * chip, 3 * every), BF16),
        pltpu.VMEM((3 * every, 3 * chip), BF16),
        pltpu.VMEM((2, rows, own, width), BF16),
        pltpu.VMEM((2, rows, own, width), F32),
        pltpu.VMEM((2, rows, own, width), BF16),
        pltpu.VMEM((3 * every, lanes), F32),
        pltpu.VMEM((side, side, pad_share, lanes), F32),
        pltpu.VMEM((side, side, pad_share, lanes), F32),
        pltpu.VMEM((side, pad_share, lanes), F32),
        pltpu.VMEM((side, pad_share, lanes), F32),
        pltpu.VMEM((pad_share, lanes), F32),
        pltpu.VMEM((pad_share, lanes), F32),
        dma((4,)),
        dma((2, side)), dma((2, side)),
        dma((2, chunks + 1)), dma((2, chunks + 1)),
        dma((2,)), dma((4,)),
        dma((3,)), dma((3,)),
        dma((2,)), dma((2,)),
        dma((chunks,)), dma((chunks,)), dma((chunks,)),
        dma((chunks,)), dma((chunks,)), dma((chunks,)),
        dma((2, chunks)), dma((2, chunks)),
        dma((4, side)), dma((4, side)),
    ]
    hbm = pl.BlockSpec(memory_space=pl.ANY)
    activated, in_own, in_other, terms = pl.pallas_call(
        functools.partial(body, side, own, share, height, width),
        out_shape=(
            jax.ShapeDtypeStruct((height, own, width), BF16),
            jax.ShapeDtypeStruct((height, own, width), F32),
            jax.ShapeDtypeStruct((height, own, width), BF16),
            jax.ShapeDtypeStruct((pad_share, lanes), F32),
        ),
        in_specs=[hbm] * 3,
        out_specs=(hbm,) * 4,
        scratch_shapes=scratch,
        compiler_params=pltpu.CompilerParams(
            collective_id=0, has_side_effects=True, vmem_limit_bytes=56 * 2**20
        ),
        name="conv_block",
    )(images[0], kernel, cotangent[0])
    input_grad = in_own + in_other.astype(F32)
    terms = terms[: 3 * share, : 3 * own].reshape(3, share, 3, own)
    kernel_grad = jnp.transpose(terms, (0, 2, 1, 3)).reshape(9, share, own)
    return activated[None], input_grad[None], kernel_grad


def solution(mesh):
    placed = (P("dp", "row", "chan", None), P(None, "dp", "chan"), P("dp", "row", "chan", None))
    return jax.shard_map(
        shards,
        mesh=mesh,
        in_specs=placed,
        out_specs=(
            P("dp", "row", "chan", None),
            P("dp", "row", "chan", None),
            P(None, "dp", "chan"),
        ),
        check_vma=False,
    )
```

```python
import functools
import math

import jax
import jax.numpy as jnp
from jax import lax
from jax.experimental import pallas as pl
from jax.experimental.pallas import tpu as pltpu
from jax.sharding import PartitionSpec as P

MESH = pl.DeviceIdType.MESH
BF16 = jnp.bfloat16
F32 = jnp.float32
ROWS = 4
PARTS = 8
HELD = 2


def round_up(x, m):
    return (x + m - 1) // m * m


def remote(src, dst, send, recv, **where):
    return pltpu.make_async_remote_copy(
        src_ref=src, dst_ref=dst, send_sem=send, recv_sem=recv, device_id=where, device_id_type=MESH
    )


def shift_right(x):
    lane = lax.broadcasted_iota(jnp.int32, x.shape, 1)
    return jnp.where(lane == 0, 0.0, pltpu.roll(x, 1, 1))


def shift_left(x):
    lane = lax.broadcasted_iota(jnp.int32, x.shape, 1)
    return jnp.where(lane == x.shape[1] - 1, 0.0, pltpu.roll(x, x.shape[1] - 1, 1))


def body(
    side, own, share, height, width,
    img, ker, cot,
    act_out, in_own, in_other, kg_out,
    xs, gs, ss, s3, acc, wk, wpk, wraw, em, wf, wb, ab, pf, pb,
    kin, kp, kr, ksum, kr2, kt, kq,
    local, wsend, wrecv, isend, irecv, hsend, hrecv, bsend, brecv,
    ssend, srecv, asend, arecv, alocal, plocal, psend, precv, csend, crecv, ksend, krecv,
):
    rows = height // 2
    chunks = rows // ROWS
    chip = 2 * own
    every = 4 * own
    pad_share = wpk.shape[1]
    lanes = s3.shape[0] // 2

    dp = lax.axis_index("dp")
    chan = lax.axis_index("chan")
    row = lax.axis_index("row")
    l = chan // 2
    c = lax.rem(chan, 2)
    sib = 2 * l + 1 - c
    other = 2 * (1 - l)
    y = dp // side
    x = lax.rem(dp, side)
    first = jnp.where(c == 0, x, y)
    second = jnp.where(c == 0, y, x)
    step_first = jnp.where(c == 0, 1, side)
    step_second = jnp.where(c == 0, side, 1)

    def on_first(k):
        f = lax.rem(first + k, side)
        return f, f * step_first + second * step_second

    def on_second(k):
        s = lax.rem(second + k, side)
        return s, first * step_first + s * step_second

    barrier = pltpu.get_barrier_semaphore()
    count = 0
    for k in range(1, 4):
        pl.semaphore_signal(barrier, inc=1, device_id={"chan": lax.rem(chan + k, 4)}, device_id_type=MESH)
        count += 1
    for g in range(4):
        pl.semaphore_signal(barrier, inc=1, device_id={"row": 1 - row, "chan": g}, device_id_type=MESH)
        count += 1
    for k in range(1, side):
        pl.semaphore_signal(barrier, inc=1, device_id={"dp": on_first(k)[1]}, device_id_type=MESH)
        pl.semaphore_signal(barrier, inc=1, device_id={"dp": on_second(k)[1]}, device_id_type=MESH)
        count += 2

    def mine(ref, first_row, n, g):
        return ref.at[pl.ds(first_row, n), pl.ds(pl.multiple_of(own * g, 16), own)]

    load_k = pltpu.make_async_copy(ker, wk, local.at[0])
    load_k.start()
    load_x = pltpu.make_async_copy(
        img.at[pl.ds((rows - 1) * c, rows + 1)], mine(xs, 1 - c, rows + 1, chan), local.at[1]
    )
    load_x.start()
    load_g = pltpu.make_async_copy(cot.at[pl.ds(rows * c, rows)], mine(gs, 0, rows, c), local.at[2])
    load_g.start()

    pl.semaphore_wait(barrier, count)

    pieces = [(rows - ROWS, ROWS + 1), (1, ROWS + 1)]
    pieces += [(ROWS * k + 2, ROWS) for k in range(1, chunks - 2)]
    pieces += [(ROWS * (chunks - 2) + 2, ROWS - 2)]
    sent = []

    def send(*args, **where):
        copy = remote(*args, **where)
        copy.start()
        sent.append(copy)

    def send_piece(to, s):
        start, n = pieces[s]
        send(
            img.at[pl.ds(rows * to + start - 1, n)], mine(xs, start, n, chan),
            isend.at[to, s], irecv.at[c, s], chan=other + to,
        )

    send_piece(0, 0)
    send_piece(1, 1)
    for to in range(2):
        send(
            img.at[pl.ds((height - 1) * (1 - row), 1)], mine(xs, (rows + 1) * row, 1, chan),
            hsend.at[to], hrecv.at[chan], row=1 - row, chan=2 * to + row,
        )
    send(
        img.at[pl.ds((rows - 1) * (1 - c), rows + 1)], mine(xs, c, rows + 1, chan),
        bsend.at[0], brecv.at[0], chan=sib,
    )
    send(cot.at[pl.ds(rows * (1 - c), rows)], mine(gs, 0, rows, c), bsend.at[1], brecv.at[1], chan=sib)
    send_piece(0, 1)
    send_piece(1, 0)
    for s in range(2, chunks):
        for to in range(2):
            send_piece(to, s)

    wpk[...] = jnp.zeros_like(wpk)
    for core in range(2):
        s3[core * lanes + 3 * own : (core + 1) * lanes, :] = jnp.zeros((lanes - 3 * own, s3.shape[1]), BF16)

    @pl.when(jnp.logical_and(c == 0, row == 0))
    def _():
        xs[0] = jnp.zeros(xs.shape[1:], BF16)
        ss[0] = jnp.zeros(ss.shape[1:], BF16)

    @pl.when(jnp.logical_and(c == 1, row == 1))
    def _():
        xs[rows + 1] = jnp.zeros(xs.shape[1:], BF16)
        ss[rows + 1] = jnp.zeros(ss.shape[1:], BF16)

    acc[...] = jnp.zeros_like(acc)
    load_k.wait()
    for b in range(3):
        for a in range(3):
            wpk[b, a * share : (a + 1) * share, 0:own] = wk[3 * a + b].astype(F32)
    wraw[c, second, first] = wpk[...].astype(BF16)

    gather = []
    for k in range(1, side):
        spot = wraw.at[c, second, first]
        copy = remote(spot, spot, wsend.at[0, k], wrecv.at[0, k], dp=on_first(k)[1])
        copy.start()
        gather.append(copy)

    spot = lax.broadcasted_iota(jnp.int32, (1, em.shape[1]), 1)
    owner = jnp.zeros_like(spot)
    for k in range(1, side * side):
        owner += (spot >= k * pad_share).astype(jnp.int32)
    within = spot - owner * pad_share
    tap = (within >= share).astype(jnp.int32) + (within >= 2 * share).astype(jnp.int32)
    target = tap * every + owner * share + within - tap * share
    target = jnp.where(within < 3 * share, target, -1)
    em[...] = (lax.broadcasted_iota(jnp.int32, em.shape, 0) == target).astype(F32).astype(BF16)

    for k in range(1, side):
        gather[k - 1].wait()
    for k in range(1, side):
        spot = wraw.at[c, second]
        copy = remote(spot, spot, wsend.at[1, k], wrecv.at[1, k], dp=on_second(k)[1])
        copy.start()
        gather.append(copy)
    for k in range(1, side):
        gather[side - 2 + k].wait()
    send(wraw.at[c], wraw.at[c], bsend.at[2], brecv.at[2], chan=sib)
    remote(wraw.at[c], wraw.at[1 - c], bsend.at[2], brecv.at[2], chan=sib).wait_recv()

    wide = 2 * wraw.shape[-1]
    fold = (
        lax.broadcasted_iota(jnp.int32, (wide, 3 * chip), 0),
        lax.broadcasted_iota(jnp.int32, (wide, 3 * chip), 1),
    )
    half = wide // 2
    core_of = (fold[0] >= half).astype(jnp.int32)
    inside = fold[0] - core_of * half
    for b in range(3):
        blocks = []
        for core in range(2):
            order = [(i, j) if core == 0 else (j, i) for i in range(side) for j in range(side)]
            blocks.append(jnp.concatenate([wraw[core, i, j, b] for i, j in order], axis=0))
        taps = jnp.dot(em[...], jnp.concatenate(blocks, axis=1), preferred_element_type=F32)
        turned = jnp.transpose(taps).astype(BF16)
        for core in range(2):
            wf[b * chip + core * own : b * chip + (core + 1) * own, :] = turned[core * half : core * half + own]
        narrow = taps.astype(BF16)
        total = jnp.zeros((every, 3 * chip), F32)
        for a in range(3):
            goal = (2 - a) * chip + core_of * own + inside
            place = jnp.logical_and(fold[1] == goal, inside < own).astype(F32).astype(BF16)
            total += jnp.dot(narrow[a * every : (a + 1) * every], place, preferred_element_type=F32)
        total = total.astype(BF16)
        for part in range(2):
            base = pl.multiple_of(b * every + chip * jnp.where(l == part, 0, 1), 16)
            wb[pl.ds(base, chip), :] = total[part * chip : (part + 1) * chip]

    load_x.wait()
    load_g.wait()
    for which, ref in ((0, mine(xs, 1 - c, rows + 1, sib)), (1, mine(gs, 0, rows, 1 - c))):
        remote(ref, ref, bsend.at[which], brecv.at[which], chan=sib).wait_recv()
    def border():
        at = pl.ds(pl.multiple_of(own * other, 16), chip)
        return remote(
            xs.at[jnp.where(c == 0, rows, 1), at], xs.at[jnp.where(c == 0, 0, rows + 1), at],
            bsend.at[3], brecv.at[3], chan=sib,
        )

    def await_rows(s, start, n):
        for of in range(2):
            ref = mine(xs, start, n, other + of)
            remote(ref, ref, isend.at[of, s], irecv.at[of, s], chan=other + of).wait_recv()

    place = 2 * row + c

    def down_copy():
        return remote(ss.at[rows], ss.at[0], ssend.at[0], srecv.at[0], row=row + c, chan=sib)

    def up_copy():
        return remote(ss.at[1], ss.at[rows + 1], ssend.at[1], srecv.at[1], row=row - (1 - c), chan=sib)

    def trade():
        return remote(acc.at[1 - c], kin, ksend.at[0, 0], krecv.at[0, 0], chan=sib)

    def plane_copies():
        made = []
        for k in range(1, side):
            f, to = on_first(k)
            made.append(remote(kp.at[f], kr.at[k], ksend.at[1, k], krecv.at[1, k], dp=to))
        return made

    def act_copies(k):
        at = pl.ds(k * ROWS, ROWS)
        to = pl.ds(rows * c + k * ROWS, ROWS)
        return (
            pltpu.make_async_copy(ab.at[c, at], act_out.at[to], alocal.at[k]),
            remote(ab.at[1 - c, at], act_out.at[to], asend.at[k], arecv.at[k], chan=sib),
        )

    def near_copies(k):
        at = pl.ds(k * ROWS, ROWS)
        to = pl.ds(rows * c + k * ROWS, ROWS)
        return (
            pltpu.make_async_copy(pf.at[c, at], in_own.at[to], plocal.at[k]),
            remote(pf.at[1 - c, at], in_own.at[to], psend.at[k], precv.at[k], chan=sib),
        )

    def far_copies(k):
        at = pl.ds(k * ROWS, ROWS)
        to = pl.ds(rows * c + k * ROWS, ROWS)
        return (
            remote(pb.at[0, at], in_other.at[to], csend.at[0, k], crecv.at[c, k], chan=other),
            remote(pb.at[1, at], in_other.at[to], csend.at[1, k], crecv.at[c, k], chan=other + 1),
        )

    def three(ref, start):
        block = ref[pl.ds(start, 3)]
        return block.reshape(3 * ref.shape[1], width)

    def forward(k):
        for pair in range(ROWS // 2):
            q = k * ROWS + 2 * pair
            right = jnp.concatenate([three(xs, q), three(xs, q + 1)], axis=1)
            taps = jnp.dot(wf[...], right, preferred_element_type=F32)
            for u in range(2):
                at = slice(u * width, (u + 1) * width)
                pre = shift_right(taps[0:chip, at]) + taps[chip : 2 * chip, at] + shift_left(taps[2 * chip :, at])
                sigma = 1.0 / (1.0 + jnp.exp(-pre))
                done = (pre * sigma).astype(BF16)
                for core in range(2):
                    ab[core, q + u] = done[core * own : (core + 1) * own]
                slope = gs[q + u].astype(F32) * sigma * (1.0 + pre * (1.0 - sigma))
                slope = slope.astype(BF16)
                ss[q + u + 1] = slope
                wide_slope = slope.astype(F32)
                turned = (shift_left(wide_slope).astype(BF16), slope, shift_right(wide_slope).astype(BF16))
                to = slice((2 * pair + u) * width, (2 * pair + u + 1) * width)
                for core in range(2):
                    for b in range(3):
                        s3[core * lanes + b * own : core * lanes + (b + 1) * own, to] = turned[b][
                            core * own : (core + 1) * own
                        ]
        left = jnp.concatenate([three(xs, k * ROWS + u) for u in range(ROWS)], axis=1)
        term = lax.dot_general(left, s3[...], (((1,), (1,)), ((), ())), preferred_element_type=F32)
        for core in range(2):
            acc[core] += term[:, core * lanes : (core + 1) * lanes]

    def backward(k):
        for pair in range(ROWS // 2):
            q = k * ROWS + 2 * pair
            right = jnp.concatenate([three(ss, q), three(ss, q + 1)], axis=1)
            taps = jnp.dot(wb[...], right, preferred_element_type=F32)
            for u in range(2):
                at = slice(u * width, (u + 1) * width)
                grad = (
                    shift_left(taps[0:every, at])
                    + taps[every : 2 * every, at]
                    + shift_right(taps[2 * every :, at])
                )
                for core in range(2):
                    pf[core, q + u] = grad[core * own : (core + 1) * own]
                    pb[core, q + u] = grad[chip + core * own : chip + (core + 1) * own].astype(BF16)

    @pl.loop(0, chunks + 3)
    def _(s):
        @pl.when(s < 2)
        def _():
            piece = jnp.where(s == 0, c, 1 - c)
            await_rows(piece, jnp.where(piece == 0, rows - ROWS, 1), ROWS + 1)

        @pl.when(s == 0)
        def _():
            border().start()
            border().wait_recv()

        @pl.when(jnp.logical_and(s == 1, c != row))
        def _():
            for g in range(4):
                ref = mine(xs, (rows + 1) * c, 1, g)
                remote(ref, ref, hsend.at[0], hrecv.at[g], row=1 - row, chan=g).wait_recv()

        @pl.when(s == chunks - 1)
        def _():
            await_rows(chunks - 1, *pieces[chunks - 1])

        @pl.when(jnp.logical_and(s > 1, s < chunks - 1))
        def _():
            await_rows(s, ROWS * (s - 1) + 2, ROWS)

        @pl.when(s < chunks)
        def _():
            k = jnp.where(s < 2, jnp.where(s == c, chunks - 1, 0), s - 1)
            forward(k)
            for copy in act_copies(k):
                copy.start()

        @pl.when(jnp.logical_and(s == c, place < 3))
        def _():
            down_copy().start()

        @pl.when(jnp.logical_and(s == 1 - c, place > 0))
        def _():
            up_copy().start()

        @pl.when(s == chunks - 1)
        def _():
            trade().start()

        @pl.when(jnp.logical_and(s == chunks + 1, place < 3))
        def _():
            up_copy().wait_recv()

        @pl.when(jnp.logical_and(s == chunks + 2, place > 0))
        def _():
            down_copy().wait_recv()

        @pl.when(s >= 3)
        def _():
            k = lax.rem(s - 2, chunks)
            backward(k)
            for copy in near_copies(k):
                copy.start()

            @pl.when(s < chunks + 3 - HELD)
            def _():
                for copy in far_copies(k):
                    copy.start()

        @pl.when(s == chunks)
        def _():
            trade().wait()
            kin[...] += acc[c]
            for i in range(side):
                for j in range(side):
                    f = jnp.where(c == 0, j, i)
                    to = jnp.where(c == 0, i, j)
                    d = i * side + j
                    for a in range(3):
                        kp[f, to, a * share : (a + 1) * share, :] = kin[
                            a * every + d * share : a * every + (d + 1) * share, :
                        ]
            for copy in plane_copies():
                copy.start()

    for copy in plane_copies():
        copy.wait()
    total = kp[first]
    for k in range(1, side):
        total += kr[k]
    ksum[...] = total
    copies = []
    for k in range(1, side):
        s, to = on_second(k)
        copy = remote(ksum.at[s], kr2.at[k], ksend.at[2, k], krecv.at[2, k], dp=to)
        copy.start()
        copies.append(copy)
    for copy in copies:
        copy.wait()
    total = ksum[second]
    for k in range(1, side):
        total += kr2[k]
    kt[...] = total
    copy = remote(kt, kq, ksend.at[3, 0], krecv.at[3, 0], row=1 - row)
    copy.start()
    for s in range(chunks + 3 - HELD, chunks + 3):
        for far in far_copies((s - 2) % chunks):
            far.start()
    copy.wait()
    kg_out[...] = kt[...] + kq[...]

    for copy in sent:
        copy.wait_send()

    border().wait_send()

    @pl.when(place < 3)
    def _():
        down_copy().wait_send()

    @pl.when(place > 0)
    def _():
        up_copy().wait_send()

    @pl.loop(0, chunks)
    def _(k):
        keep, give = act_copies(k)
        keep.wait()
        give.wait()
        keep, give = near_copies(k)
        keep.wait()
        give.wait()
        for copy in far_copies(k):
            copy.wait_send()
        for of in range(2):
            ref = in_other.at[pl.ds(rows * of + k * ROWS, ROWS)]
            remote(ref, ref, csend.at[of, k], crecv.at[of, k], chan=other + of).wait_recv()


def finish(own, share, act, in_own, in_other, terms, act_out, grad_out, kg_out, grad, kg, sems):
    keep = pltpu.make_async_copy(act, act_out, sems.at[0])
    keep.start()
    step = in_own.shape[0] // PARTS
    copies = []
    for p in range(PARTS):
        at = pl.ds(p * step, step)
        grad[at] = in_own[at] + in_other[at].astype(F32)
        copy = pltpu.make_async_copy(grad.at[at], grad_out.at[at], sems.at[2 + p])
        copy.start()
        copies.append(copy)
    for a in range(3):
        for b in range(3):
            kg[3 * a + b] = terms[a * share : (a + 1) * share, b * own : (b + 1) * own]
    last = pltpu.make_async_copy(kg, kg_out, sems.at[1])
    last.start()
    keep.wait()
    for copy in copies:
        copy.wait()
    last.wait()


def shards(images, kernel, cotangent):
    _, height, own, width = images.shape
    share = kernel.shape[1]
    side = math.isqrt(lax.axis_size("dp"))
    rows = height // 2
    chunks = rows // ROWS
    chip, every = 2 * own, 4 * own
    pad_share = round_up(3 * share, 16)
    pad_own = round_up(own, 128)
    lanes = round_up(3 * own, 128)
    dma = pltpu.SemaphoreType.DMA
    scratch = [
        pltpu.VMEM((rows + 2, every, width), BF16),
        pltpu.VMEM((rows, chip, width), BF16),
        pltpu.VMEM((rows + 2, chip, width), BF16),
        pltpu.VMEM((2 * lanes, ROWS * width), BF16),
        pltpu.VMEM((2, 3 * every, lanes), F32),
        pltpu.VMEM(kernel.shape, BF16),
        pltpu.VMEM((3, pad_share, pad_own), F32),
        pltpu.VMEM((2, side, side, 3, pad_share, pad_own), BF16),
        pltpu.VMEM((3 * every, side * side * pad_share), BF16),
        pltpu.VMEM((3 * chip, 3 * every), BF16),
        pltpu.VMEM((3 * every, 3 * chip), BF16),
        pltpu.VMEM((2, rows, own, width), BF16),
        pltpu.VMEM((2, rows, own, width), F32),
        pltpu.VMEM((2, rows, own, width), BF16),
        pltpu.VMEM((3 * every, lanes), F32),
        pltpu.VMEM((side, side, pad_share, lanes), F32),
        pltpu.VMEM((side, side, pad_share, lanes), F32),
        pltpu.VMEM((side, pad_share, lanes), F32),
        pltpu.VMEM((side, pad_share, lanes), F32),
        pltpu.VMEM((pad_share, lanes), F32),
        pltpu.VMEM((pad_share, lanes), F32),
        dma((3,)),
        dma((2, side)), dma((2, side)),
        dma((2, chunks)), dma((2, chunks)),
        dma((2,)), dma((4,)),
        dma((4,)), dma((4,)),
        dma((2,)), dma((2,)),
        dma((chunks,)), dma((chunks,)), dma((chunks,)),
        dma((chunks,)), dma((chunks,)), dma((chunks,)),
        dma((2, chunks)), dma((2, chunks)),
        dma((4, side)), dma((4, side)),
    ]
    hbm = pl.BlockSpec(memory_space=pl.ANY)
    vmem = pl.BlockSpec(memory_space=pltpu.VMEM)
    activated, in_own, in_other, terms = pl.pallas_call(
        functools.partial(body, side, own, share, height, width),
        out_shape=(
            pltpu.VMEM((height, own, width), BF16),
            pltpu.VMEM((height, own, width), F32),
            pltpu.VMEM((height, own, width), BF16),
            pltpu.VMEM((pad_share, lanes), F32),
        ),
        in_specs=[hbm] * 3,
        out_specs=(vmem,) * 4,
        scratch_shapes=scratch,
        compiler_params=pltpu.CompilerParams(
            collective_id=0, has_side_effects=True, vmem_limit_bytes=44 * 2**20
        ),
        name="conv_block",
    )(images[0], kernel, cotangent[0])
    activated, input_grad, kernel_grad = pl.pallas_call(
        functools.partial(finish, own, share),
        out_shape=(
            jax.ShapeDtypeStruct((height, own, width), BF16),
            jax.ShapeDtypeStruct((height, own, width), F32),
            jax.ShapeDtypeStruct((9, share, own), F32),
        ),
        in_specs=[vmem] * 4,
        out_specs=(hbm, hbm, hbm),
        scratch_shapes=[
            pltpu.VMEM((height, own, width), F32),
            pltpu.VMEM((9, share, own), F32),
            dma((2 + PARTS,)),
        ],
        compiler_params=pltpu.CompilerParams(vmem_limit_bytes=16 * 2**20),
        name="results",
    )(activated, in_own, in_other, terms)
    return activated[None], input_grad[None], kernel_grad


def solution(mesh):
    placed = (P("dp", "row", "chan", None), P(None, "dp", "chan"), P("dp", "row", "chan", None))
    return jax.shard_map(
        shards,
        mesh=mesh,
        in_specs=placed,
        out_specs=(
            P("dp", "row", "chan", None),
            P("dp", "row", "chan", None),
            P(None, "dp", "chan"),
        ),
        check_vma=False,
    )
```

```python
import functools
import math

import jax
import jax.numpy as jnp
from jax import lax
from jax.experimental import pallas as pl
from jax.experimental.pallas import tpu as pltpu
from jax.sharding import PartitionSpec as P

MESH = pl.DeviceIdType.MESH
BF16 = jnp.bfloat16
F32 = jnp.float32
ROWS = 4
PARTS = 4
HELD = 1


def round_up(x, m):
    return (x + m - 1) // m * m


def remote(src, dst, send, recv, **where):
    return pltpu.make_async_remote_copy(
        src_ref=src, dst_ref=dst, send_sem=send, recv_sem=recv, device_id=where, device_id_type=MESH
    )


def shift_right(x):
    lane = lax.broadcasted_iota(jnp.int32, x.shape, 1)
    return jnp.where(lane == 0, 0.0, pltpu.roll(x, 1, 1))


def shift_left(x):
    lane = lax.broadcasted_iota(jnp.int32, x.shape, 1)
    return jnp.where(lane == x.shape[1] - 1, 0.0, pltpu.roll(x, x.shape[1] - 1, 1))


def body(
    side, own, share, height, width,
    img, ker, cot,
    act_out, grad_out, kg_out,
    xs, gs, ss, s3, acc, wk, wpk, wraw, em, wf, wb, ab, pf, pb,
    arrived, kin, kp, kr, ksum, kr2, kt, kq,
    local, wsend, wrecv, isend, irecv, hsend, hrecv, bsend, brecv,
    ssend, srecv, asend, arecv, alocal, plocal, psend, precv, csend, crecv, ksend, krecv,
):
    rows = height // 2
    chunks = rows // ROWS
    chip = 2 * own
    every = 4 * own
    pad_share = wpk.shape[1]
    lanes = s3.shape[0] // 2

    dp = lax.axis_index("dp")
    chan = lax.axis_index("chan")
    row = lax.axis_index("row")
    l = chan // 2
    c = lax.rem(chan, 2)
    sib = 2 * l + 1 - c
    other = 2 * (1 - l)
    y = dp // side
    x = lax.rem(dp, side)
    first = jnp.where(c == 0, x, y)
    second = jnp.where(c == 0, y, x)
    step_first = jnp.where(c == 0, 1, side)
    step_second = jnp.where(c == 0, side, 1)

    def on_first(k):
        f = lax.rem(first + k, side)
        return f, f * step_first + second * step_second

    def on_second(k):
        s = lax.rem(second + k, side)
        return s, first * step_first + s * step_second

    barrier = pltpu.get_barrier_semaphore()
    count = 0
    for k in range(1, 4):
        pl.semaphore_signal(barrier, inc=1, device_id={"chan": lax.rem(chan + k, 4)}, device_id_type=MESH)
        count += 1
    for g in range(4):
        pl.semaphore_signal(barrier, inc=1, device_id={"row": 1 - row, "chan": g}, device_id_type=MESH)
        count += 1
    for k in range(1, side):
        pl.semaphore_signal(barrier, inc=1, device_id={"dp": on_first(k)[1]}, device_id_type=MESH)
        pl.semaphore_signal(barrier, inc=1, device_id={"dp": on_second(k)[1]}, device_id_type=MESH)
        count += 2

    def mine(ref, first_row, n, g):
        return ref.at[pl.ds(first_row, n), pl.ds(pl.multiple_of(own * g, 16), own)]

    load_k = pltpu.make_async_copy(ker, wk, local.at[0])
    load_k.start()
    load_x = pltpu.make_async_copy(
        img.at[pl.ds((rows - 1) * c, rows + 1)], mine(xs, 1 - c, rows + 1, chan), local.at[1]
    )
    load_x.start()
    load_g = pltpu.make_async_copy(cot.at[pl.ds(rows * c, rows)], mine(gs, 0, rows, c), local.at[2])
    load_g.start()

    pl.semaphore_wait(barrier, count)

    pieces = [(rows - ROWS, ROWS + 1), (1, ROWS + 1)]
    pieces += [(ROWS * k + 2, ROWS) for k in range(1, chunks - 2)]
    pieces += [(ROWS * (chunks - 2) + 2, ROWS - 2)]
    sent = []

    def send(*args, **where):
        copy = remote(*args, **where)
        copy.start()
        sent.append(copy)

    def send_piece(to, s):
        start, n = pieces[s]
        send(
            img.at[pl.ds(rows * to + start - 1, n)], mine(xs, start, n, chan),
            isend.at[to, s], irecv.at[c, s], chan=other + to,
        )

    send_piece(0, 0)
    send_piece(1, 1)
    for to in range(2):
        send(
            img.at[pl.ds((height - 1) * (1 - row), 1)], mine(xs, (rows + 1) * row, 1, chan),
            hsend.at[to], hrecv.at[chan], row=1 - row, chan=2 * to + row,
        )
    send(
        img.at[pl.ds((rows - 1) * (1 - c), rows + 1)], mine(xs, c, rows + 1, chan),
        bsend.at[0], brecv.at[0], chan=sib,
    )
    send(cot.at[pl.ds(rows * (1 - c), rows)], mine(gs, 0, rows, c), bsend.at[1], brecv.at[1], chan=sib)
    send_piece(0, 1)
    send_piece(1, 0)
    for s in range(2, chunks):
        for to in range(2):
            send_piece(to, s)

    wpk[...] = jnp.zeros_like(wpk)
    for core in range(2):
        s3[core * lanes + 3 * own : (core + 1) * lanes, :] = jnp.zeros((lanes - 3 * own, s3.shape[1]), BF16)

    @pl.when(jnp.logical_and(c == 0, row == 0))
    def _():
        xs[0] = jnp.zeros(xs.shape[1:], BF16)
        ss[0] = jnp.zeros(ss.shape[1:], BF16)

    @pl.when(jnp.logical_and(c == 1, row == 1))
    def _():
        xs[rows + 1] = jnp.zeros(xs.shape[1:], BF16)
        ss[rows + 1] = jnp.zeros(ss.shape[1:], BF16)

    acc[...] = jnp.zeros_like(acc)
    load_k.wait()
    for b in range(3):
        for a in range(3):
            wpk[b, a * share : (a + 1) * share, 0:own] = wk[3 * a + b].astype(F32)
    wraw[c, second, first] = wpk[...].astype(BF16)

    gather = []
    for k in range(1, side):
        spot = wraw.at[c, second, first]
        copy = remote(spot, spot, wsend.at[0, k], wrecv.at[0, k], dp=on_first(k)[1])
        copy.start()
        gather.append(copy)

    spot = lax.broadcasted_iota(jnp.int32, (1, em.shape[1]), 1)
    owner = jnp.zeros_like(spot)
    for k in range(1, side * side):
        owner += (spot >= k * pad_share).astype(jnp.int32)
    within = spot - owner * pad_share
    tap = (within >= share).astype(jnp.int32) + (within >= 2 * share).astype(jnp.int32)
    target = tap * every + owner * share + within - tap * share
    target = jnp.where(within < 3 * share, target, -1)
    em[...] = (lax.broadcasted_iota(jnp.int32, em.shape, 0) == target).astype(F32).astype(BF16)

    for k in range(1, side):
        gather[k - 1].wait()
    for k in range(1, side):
        spot = wraw.at[c, second]
        copy = remote(spot, spot, wsend.at[1, k], wrecv.at[1, k], dp=on_second(k)[1])
        copy.start()
        gather.append(copy)
    for k in range(1, side):
        gather[side - 2 + k].wait()
    send(wraw.at[c], wraw.at[c], bsend.at[2], brecv.at[2], chan=sib)
    remote(wraw.at[c], wraw.at[1 - c], bsend.at[2], brecv.at[2], chan=sib).wait_recv()

    wide = 2 * wraw.shape[-1]
    fold = (
        lax.broadcasted_iota(jnp.int32, (wide, 3 * chip), 0),
        lax.broadcasted_iota(jnp.int32, (wide, 3 * chip), 1),
    )
    half = wide // 2
    core_of = (fold[0] >= half).astype(jnp.int32)
    inside = fold[0] - core_of * half
    for b in range(3):
        blocks = []
        for core in range(2):
            order = [(i, j) if core == 0 else (j, i) for i in range(side) for j in range(side)]
            blocks.append(jnp.concatenate([wraw[core, i, j, b] for i, j in order], axis=0))
        taps = jnp.dot(em[...], jnp.concatenate(blocks, axis=1), preferred_element_type=F32)
        turned = jnp.transpose(taps).astype(BF16)
        for core in range(2):
            wf[b * chip + core * own : b * chip + (core + 1) * own, :] = turned[core * half : core * half + own]
        narrow = taps.astype(BF16)
        total = jnp.zeros((every, 3 * chip), F32)
        for a in range(3):
            goal = (2 - a) * chip + core_of * own + inside
            place = jnp.logical_and(fold[1] == goal, inside < own).astype(F32).astype(BF16)
            total += jnp.dot(narrow[a * every : (a + 1) * every], place, preferred_element_type=F32)
        total = total.astype(BF16)
        for part in range(2):
            base = pl.multiple_of(b * every + chip * jnp.where(l == part, 0, 1), 16)
            wb[pl.ds(base, chip), :] = total[part * chip : (part + 1) * chip]

    load_x.wait()
    load_g.wait()
    for which, ref in ((0, mine(xs, 1 - c, rows + 1, sib)), (1, mine(gs, 0, rows, 1 - c))):
        remote(ref, ref, bsend.at[which], brecv.at[which], chan=sib).wait_recv()
    def border():
        at = pl.ds(pl.multiple_of(own * other, 16), chip)
        return remote(
            xs.at[jnp.where(c == 0, rows, 1), at], xs.at[jnp.where(c == 0, 0, rows + 1), at],
            bsend.at[3], brecv.at[3], chan=sib,
        )

    def await_rows(s, start, n):
        for of in range(2):
            ref = mine(xs, start, n, other + of)
            remote(ref, ref, isend.at[of, s], irecv.at[of, s], chan=other + of).wait_recv()

    place = 2 * row + c

    def down_copy():
        return remote(ss.at[rows], ss.at[0], ssend.at[0], srecv.at[0], row=row + c, chan=sib)

    def up_copy():
        return remote(ss.at[1], ss.at[rows + 1], ssend.at[1], srecv.at[1], row=row - (1 - c), chan=sib)

    def trade():
        return remote(acc.at[1 - c], kin, ksend.at[0, 0], krecv.at[0, 0], chan=sib)

    def plane_copies():
        made = []
        for k in range(1, side):
            f, to = on_first(k)
            made.append(remote(kp.at[f], kr.at[k], ksend.at[1, k], krecv.at[1, k], dp=to))
        return made

    def act_copies(k):
        at = pl.ds(k * ROWS, ROWS)
        to = pl.ds(rows * c + k * ROWS, ROWS)
        return (
            pltpu.make_async_copy(ab.at[c, at], act_out.at[to], alocal.at[k]),
            remote(ab.at[1 - c, at], act_out.at[to], asend.at[k], arecv.at[k], chan=sib),
        )

    def near_copies(k):
        at = pl.ds(k * ROWS, ROWS)
        to = pl.ds(rows * c + k * ROWS, ROWS)
        return (
            pltpu.make_async_copy(pf.at[c, at], grad_out.at[to], plocal.at[k]),
            remote(pf.at[1 - c, at], grad_out.at[to], psend.at[k], precv.at[k], chan=sib),
        )

    def far_copies(k):
        at = pl.ds(k * ROWS, ROWS)
        to = pl.ds(rows * c + k * ROWS, ROWS)
        return (
            remote(pb.at[0, at], arrived.at[to], csend.at[0, k], crecv.at[c, k], chan=other),
            remote(pb.at[1, at], arrived.at[to], csend.at[1, k], crecv.at[c, k], chan=other + 1),
        )

    def three(ref, start):
        block = ref[pl.ds(start, 3)]
        return block.reshape(3 * ref.shape[1], width)

    def forward(k):
        for pair in range(ROWS // 2):
            q = k * ROWS + 2 * pair
            right = jnp.concatenate([three(xs, q), three(xs, q + 1)], axis=1)
            taps = jnp.dot(wf[...], right, preferred_element_type=F32)
            for u in range(2):
                at = slice(u * width, (u + 1) * width)
                pre = shift_right(taps[0:chip, at]) + taps[chip : 2 * chip, at] + shift_left(taps[2 * chip :, at])
                sigma = 1.0 / (1.0 + jnp.exp(-pre))
                done = (pre * sigma).astype(BF16)
                for core in range(2):
                    ab[core, q + u] = done[core * own : (core + 1) * own]
                slope = gs[q + u].astype(F32) * sigma * (1.0 + pre * (1.0 - sigma))
                slope = slope.astype(BF16)
                ss[q + u + 1] = slope
                wide_slope = slope.astype(F32)
                turned = (shift_left(wide_slope).astype(BF16), slope, shift_right(wide_slope).astype(BF16))
                to = slice((2 * pair + u) * width, (2 * pair + u + 1) * width)
                for core in range(2):
                    for b in range(3):
                        s3[core * lanes + b * own : core * lanes + (b + 1) * own, to] = turned[b][
                            core * own : (core + 1) * own
                        ]
        left = jnp.concatenate([three(xs, k * ROWS + u) for u in range(ROWS)], axis=1)
        term = lax.dot_general(left, s3[...], (((1,), (1,)), ((), ())), preferred_element_type=F32)
        for core in range(2):
            acc[core] += term[:, core * lanes : (core + 1) * lanes]

    def backward(k):
        for pair in range(ROWS // 2):
            q = k * ROWS + 2 * pair
            right = jnp.concatenate([three(ss, q), three(ss, q + 1)], axis=1)
            taps = jnp.dot(wb[...], right, preferred_element_type=F32)
            for u in range(2):
                at = slice(u * width, (u + 1) * width)
                grad = (
                    shift_left(taps[0:every, at])
                    + taps[every : 2 * every, at]
                    + shift_right(taps[2 * every :, at])
                )
                for core in range(2):
                    pf[core, q + u] = grad[core * own : (core + 1) * own]
                    pb[core, q + u] = grad[chip + core * own : chip + (core + 1) * own].astype(BF16)

    @pl.loop(0, chunks + 3)
    def _(s):
        @pl.when(s < 2)
        def _():
            piece = jnp.where(s == 0, c, 1 - c)
            await_rows(piece, jnp.where(piece == 0, rows - ROWS, 1), ROWS + 1)

        @pl.when(s == 0)
        def _():
            border().start()
            border().wait_recv()

        @pl.when(jnp.logical_and(s == 1, c != row))
        def _():
            for g in range(4):
                ref = mine(xs, (rows + 1) * c, 1, g)
                remote(ref, ref, hsend.at[0], hrecv.at[g], row=1 - row, chan=g).wait_recv()

        @pl.when(s == chunks - 1)
        def _():
            await_rows(chunks - 1, *pieces[chunks - 1])

        @pl.when(jnp.logical_and(s > 1, s < chunks - 1))
        def _():
            await_rows(s, ROWS * (s - 1) + 2, ROWS)

        @pl.when(s < chunks)
        def _():
            k = jnp.where(s < 2, jnp.where(s == c, chunks - 1, 0), s - 1)
            forward(k)
            for copy in act_copies(k):
                copy.start()

        @pl.when(jnp.logical_and(s == c, place < 3))
        def _():
            down_copy().start()

        @pl.when(jnp.logical_and(s == 1 - c, place > 0))
        def _():
            up_copy().start()

        @pl.when(s == chunks - 1)
        def _():
            trade().start()

        @pl.when(jnp.logical_and(s == chunks + 1, place < 3))
        def _():
            up_copy().wait_recv()

        @pl.when(jnp.logical_and(s == chunks + 2, place > 0))
        def _():
            down_copy().wait_recv()

        @pl.when(s >= 3)
        def _():
            k = lax.rem(s - 2, chunks)
            backward(k)
            for copy in near_copies(k):
                copy.start()

            @pl.when(s < chunks + 3 - HELD)
            def _():
                for copy in far_copies(k):
                    copy.start()

        @pl.when(s == chunks - 1)
        def _():
            trade().wait()
            kin[...] += acc[c]
            for i in range(side):
                for j in range(side):
                    f = jnp.where(c == 0, j, i)
                    to = jnp.where(c == 0, i, j)
                    d = i * side + j
                    for a in range(3):
                        kp[f, to, a * share : (a + 1) * share, :] = kin[
                            a * every + d * share : a * every + (d + 1) * share, :
                        ]
            for copy in plane_copies():
                copy.start()

    for copy in plane_copies():
        copy.wait()
    total = kp[first]
    for k in range(1, side):
        total += kr[k]
    ksum[...] = total
    copies = []
    for k in range(1, side):
        s, to = on_second(k)
        copy = remote(ksum.at[s], kr2.at[k], ksend.at[2, k], krecv.at[2, k], dp=to)
        copy.start()
        copies.append(copy)
    for copy in copies:
        copy.wait()
    total = ksum[second]
    for k in range(1, side):
        total += kr2[k]
    kt[...] = total
    copy = remote(kt, kq, ksend.at[3, 0], krecv.at[3, 0], row=1 - row)
    copy.start()
    for s in range(chunks + 3 - HELD, chunks + 3):
        for far in far_copies((s - 2) % chunks):
            far.start()
    copy.wait()
    kg_out[...] = kt[...] + kq[...]

    @pl.loop(1, chunks + 1)
    def _(k):
        k = lax.rem(k, chunks)
        for copy in near_copies(k):
            copy.wait()
        for of in range(2):
            at = pl.ds(rows * of + k * ROWS, ROWS)
            ref = arrived.at[at]
            remote(ref, ref, csend.at[of, k], crecv.at[of, k], chan=other + of).wait_recv()
            grad_out[at] += arrived[at].astype(F32)

    for copy in sent:
        copy.wait_send()
    border().wait_send()

    @pl.when(place < 3)
    def _():
        down_copy().wait_send()

    @pl.when(place > 0)
    def _():
        up_copy().wait_send()

    @pl.loop(0, chunks)
    def _(k):
        for copy in act_copies(k):
            copy.wait()
        for copy in far_copies(k):
            copy.wait_send()


def finish(own, share, act, grad, terms, act_out, grad_out, kg_out, kg, sems):
    step = grad.shape[0] // PARTS
    copies = []
    for p in range(PARTS):
        at = pl.ds(p * step, step)
        copies.append(pltpu.make_async_copy(grad.at[at], grad_out.at[at], sems.at[p, 0]))
        copies.append(pltpu.make_async_copy(act.at[at], act_out.at[at], sems.at[p, 1]))
    for copy in copies:
        copy.start()
    for a in range(3):
        for b in range(3):
            kg[3 * a + b] = terms[a * share : (a + 1) * share, b * own : (b + 1) * own]
    last = pltpu.make_async_copy(kg, kg_out, sems.at[PARTS, 0])
    last.start()
    for copy in copies:
        copy.wait()
    last.wait()


def shards(images, kernel, cotangent):
    _, height, own, width = images.shape
    share = kernel.shape[1]
    side = math.isqrt(lax.axis_size("dp"))
    rows = height // 2
    chunks = rows // ROWS
    chip, every = 2 * own, 4 * own
    pad_share = round_up(3 * share, 16)
    pad_own = round_up(own, 128)
    lanes = round_up(3 * own, 128)
    dma = pltpu.SemaphoreType.DMA
    scratch = [
        pltpu.VMEM((rows + 2, every, width), BF16),
        pltpu.VMEM((rows, chip, width), BF16),
        pltpu.VMEM((rows + 2, chip, width), BF16),
        pltpu.VMEM((2 * lanes, ROWS * width), BF16),
        pltpu.VMEM((2, 3 * every, lanes), F32),
        pltpu.VMEM(kernel.shape, BF16),
        pltpu.VMEM((3, pad_share, pad_own), F32),
        pltpu.VMEM((2, side, side, 3, pad_share, pad_own), BF16),
        pltpu.VMEM((3 * every, side * side * pad_share), BF16),
        pltpu.VMEM((3 * chip, 3 * every), BF16),
        pltpu.VMEM((3 * every, 3 * chip), BF16),
        pltpu.VMEM((2, rows, own, width), BF16),
        pltpu.VMEM((2, rows, own, width), F32),
        pltpu.VMEM((2, rows, own, width), BF16),
        pltpu.VMEM((height, own, width), BF16),
        pltpu.VMEM((3 * every, lanes), F32),
        pltpu.VMEM((side, side, pad_share, lanes), F32),
        pltpu.VMEM((side, side, pad_share, lanes), F32),
        pltpu.VMEM((side, pad_share, lanes), F32),
        pltpu.VMEM((side, pad_share, lanes), F32),
        pltpu.VMEM((pad_share, lanes), F32),
        pltpu.VMEM((pad_share, lanes), F32),
        dma((3,)),
        dma((2, side)), dma((2, side)),
        dma((2, chunks)), dma((2, chunks)),
        dma((2,)), dma((4,)),
        dma((4,)), dma((4,)),
        dma((2,)), dma((2,)),
        dma((chunks,)), dma((chunks,)), dma((chunks,)),
        dma((chunks,)), dma((chunks,)), dma((chunks,)),
        dma((2, chunks)), dma((2, chunks)),
        dma((4, side)), dma((4, side)),
    ]
    hbm = pl.BlockSpec(memory_space=pl.ANY)
    vmem = pl.BlockSpec(memory_space=pltpu.VMEM)
    activated, input_grad, terms = pl.pallas_call(
        functools.partial(body, side, own, share, height, width),
        out_shape=(
            pltpu.VMEM((height, own, width), BF16),
            pltpu.VMEM((height, own, width), F32),
            pltpu.VMEM((pad_share, lanes), F32),
        ),
        in_specs=[hbm] * 3,
        out_specs=(vmem,) * 3,
        scratch_shapes=scratch,
        compiler_params=pltpu.CompilerParams(
            collective_id=0, has_side_effects=True, vmem_limit_bytes=56 * 2**20
        ),
        name="conv_block",
    )(images[0], kernel, cotangent[0])
    activated, input_grad, kernel_grad = pl.pallas_call(
        functools.partial(finish, own, share),
        out_shape=(
            jax.ShapeDtypeStruct((height, own, width), BF16),
            jax.ShapeDtypeStruct((height, own, width), F32),
            jax.ShapeDtypeStruct((9, share, own), F32),
        ),
        in_specs=[vmem] * 3,
        out_specs=(hbm, hbm, hbm),
        scratch_shapes=[pltpu.VMEM((9, share, own), F32), dma((PARTS + 1, 2))],
        compiler_params=pltpu.CompilerParams(vmem_limit_bytes=16 * 2**20),
        name="results",
    )(activated, input_grad, terms)
    return activated[None], input_grad[None], kernel_grad


def solution(mesh):
    placed = (P("dp", "row", "chan", None), P(None, "dp", "chan"), P("dp", "row", "chan", None))
    return jax.shard_map(
        shards,
        mesh=mesh,
        in_specs=placed,
        out_specs=(
            P("dp", "row", "chan", None),
            P("dp", "row", "chan", None),
            P(None, "dp", "chan"),
        ),
        check_vma=False,
    )
```

```python
import functools
import math

import jax
import jax.numpy as jnp
from jax import lax
from jax.experimental import pallas as pl
from jax.experimental.pallas import tpu as pltpu
from jax.sharding import PartitionSpec as P

MESH = pl.DeviceIdType.MESH
BF16 = jnp.bfloat16
F32 = jnp.float32
ROWS = 4
PARTS = 4
HELD = 1


def round_up(x, m):
    return (x + m - 1) // m * m


def remote(src, dst, send, recv, **where):
    return pltpu.make_async_remote_copy(
        src_ref=src, dst_ref=dst, send_sem=send, recv_sem=recv, device_id=where, device_id_type=MESH
    )


def shift_right(x):
    lane = lax.broadcasted_iota(jnp.int32, x.shape, 1)
    return jnp.where(lane == 0, 0.0, pltpu.roll(x, 1, 1))


def shift_left(x):
    lane = lax.broadcasted_iota(jnp.int32, x.shape, 1)
    return jnp.where(lane == x.shape[1] - 1, 0.0, pltpu.roll(x, x.shape[1] - 1, 1))


def body(
    side, own, share, height, width,
    img, ker, cot,
    act_out, grad_out, kg_out,
    xs, gs, ss, s3, acc, wk, wpk, wraw, em, wf, wb, ab, pf, pb,
    arrived, kin, kp, kr, ksum, kr2, kt, kq,
    local, wsend, wrecv, isend, irecv, hsend, hrecv, bsend, brecv,
    ssend, srecv, asend, arecv, alocal, plocal, psend, precv, csend, crecv, ksend, krecv,
    fsend, frecv, near_ready, far_ready,
):
    rows = height // 2
    chunks = rows // ROWS
    chip = 2 * own
    every = 4 * own
    pad_share = wpk.shape[0]
    lanes = s3.shape[1] // 2

    dp = lax.axis_index("dp")
    chan = lax.axis_index("chan")
    row = lax.axis_index("row")
    l = chan // 2
    c = lax.rem(chan, 2)
    sib = 2 * l + 1 - c
    other = 2 * (1 - l)
    y = dp // side
    x = lax.rem(dp, side)
    first = jnp.where(c == 0, x, y)
    second = jnp.where(c == 0, y, x)
    step_first = jnp.where(c == 0, 1, side)
    step_second = jnp.where(c == 0, side, 1)

    def on_first(k):
        f = lax.rem(first + k, side)
        return f, f * step_first + second * step_second

    def on_second(k):
        s = lax.rem(second + k, side)
        return s, first * step_first + s * step_second

    barrier = pltpu.get_barrier_semaphore()
    pl.semaphore_signal(barrier, inc=1, device_id={"chan": other + 1}, device_id_type=MESH)

    @pl.when(c == 0)
    def _():
        pl.semaphore_signal(barrier, inc=1, device_id={"chan": sib}, device_id_type=MESH)

    for to in range(2):
        pl.semaphore_signal(barrier, inc=1, device_id={"row": 1 - row, "chan": 2 * to}, device_id_type=MESH)
    for k in range(1, side):
        for to in (on_first(k)[1], on_second(k)[1]):
            pl.semaphore_signal(barrier, inc=1, device_id={"dp": to, "chan": 2 * l}, device_id_type=MESH)

    def mine(ref, first_row, n, g):
        return ref.at[pl.ds(first_row, n), pl.ds(pl.multiple_of(own * g, 16), own)]

    load_k = pltpu.make_async_copy(ker, wk, local.at[0])
    load_k.start()
    load_x = pltpu.make_async_copy(
        img.at[pl.ds((rows - 1) * c, rows + 1)], mine(xs, 1 - c, rows + 1, chan), local.at[1]
    )
    load_x.start()
    load_g = pltpu.make_async_copy(cot.at[pl.ds(rows * c, rows)], mine(gs, 0, rows, c), local.at[2])
    load_g.start()

    @pl.when(c == 1)
    def _():
        pl.semaphore_wait(barrier, 3)
        pl.semaphore_signal(near_ready, inc=1, device_id={"chan": sib}, device_id_type=MESH)

    @pl.when(c == 0)
    def _():
        pl.semaphore_wait(near_ready, 1)

    pieces = [(rows - ROWS, ROWS + 1), (1, ROWS + 1)]
    pieces += [(ROWS * k + 2, ROWS) for k in range(1, chunks - 2)]
    pieces += [(ROWS * (chunks - 2) + 2, ROWS - 2)]
    sent = []

    def send(*args, **where):
        copy = remote(*args, **where)
        copy.start()
        sent.append(copy)

    def send_piece(to, s):
        start, n = pieces[s]
        send(
            img.at[pl.ds(rows * to + start - 1, n)], mine(xs, start, n, chan),
            isend.at[to, s], irecv.at[c, s], chan=other + to,
        )

    send_piece(0, 0)
    send_piece(1, 1)
    send(
        img.at[pl.ds((rows - 1) * (1 - c), rows + 1)], mine(xs, c, rows + 1, chan),
        bsend.at[0], brecv.at[0], chan=sib,
    )
    send(cot.at[pl.ds(rows * (1 - c), rows)], mine(gs, 0, rows, c), bsend.at[1], brecv.at[1], chan=sib)
    send_piece(0, 1)
    send_piece(1, 0)
    for to in range(2):
        send_piece(to, 2)

    wpk[...] = jnp.zeros_like(wpk)
    load_k.wait()
    for b in range(3):
        for a in range(3):
            wpk[a * share : (a + 1) * share, b * own : (b + 1) * own] = wk[3 * a + b].astype(F32)
    wraw[c, second, first] = wpk[...].astype(BF16)

    @pl.when(c == 0)
    def _():
        pl.semaphore_wait(barrier, 4 + 4 * (side - 1))
        pl.semaphore_signal(far_ready, inc=1, device_id={"chan": sib}, device_id_type=MESH)

    @pl.when(c == 1)
    def _():
        pl.semaphore_wait(far_ready, 1)

    gather = []
    for k in range(1, side):
        spot = wraw.at[c, second, first]
        copy = remote(spot, spot, wsend.at[0, k], wrecv.at[0, k], dp=on_first(k)[1])
        copy.start()
        gather.append(copy)

    for to in range(2):
        send(
            img.at[pl.ds((height - 1) * (1 - row), 1)], mine(xs, (rows + 1) * row, 1, chan),
            hsend.at[to], hrecv.at[chan], row=1 - row, chan=2 * to + row,
        )
    for s in range(3, chunks):
        for to in range(2):
            send_piece(to, s)

    for core in range(2):
        s3[:, core * lanes + 3 * own : (core + 1) * lanes, :] = jnp.zeros((chunks, lanes - 3 * own, s3.shape[2]), BF16)

    @pl.when(jnp.logical_and(c == 0, row == 0))
    def _():
        xs[0] = jnp.zeros(xs.shape[1:], BF16)
        ss[0] = jnp.zeros(ss.shape[1:], BF16)

    @pl.when(jnp.logical_and(c == 1, row == 1))
    def _():
        xs[rows + 1] = jnp.zeros(xs.shape[1:], BF16)
        ss[rows + 1] = jnp.zeros(ss.shape[1:], BF16)

    acc[...] = jnp.zeros_like(acc)
    spot = lax.broadcasted_iota(jnp.int32, (1, em.shape[1]), 1)
    owner = jnp.zeros_like(spot)
    for k in range(1, side * side):
        owner += (spot >= k * pad_share).astype(jnp.int32)
    within = spot - owner * pad_share
    tap = (within >= share).astype(jnp.int32) + (within >= 2 * share).astype(jnp.int32)
    target = tap * every + owner * share + within - tap * share
    target = jnp.where(within < 3 * share, target, -1)
    em[...] = (lax.broadcasted_iota(jnp.int32, em.shape, 0) == target).astype(F32).astype(BF16)

    for copy in gather:
        copy.wait()
    spot = wraw.at[c, second]
    gather = [remote(spot, spot, wsend.at[1, k], wrecv.at[1, k], dp=on_second(k)[1]) for k in range(1, side)]
    for copy in gather:
        copy.start()
    send(spot, spot, fsend.at[0], frecv.at[0], chan=sib)
    for k in range(1, side):
        gather[k - 1].wait()
        spot = wraw.at[c, lax.rem(second + side - k, side)]
        send(spot, spot, fsend.at[k], frecv.at[k], chan=sib)
    for k in range(side):
        spot = wraw.at[1 - c, k]
        remote(spot, spot, fsend.at[k], frecv.at[k], chan=sib).wait_recv()

    for core in range(2):
        order = [(i, j) if core == 0 else (j, i) for i in range(side) for j in range(side)]
        blocks = jnp.concatenate([wraw[core, i, j] for i, j in order], axis=0)
        taps = jnp.dot(em[...], blocks, preferred_element_type=F32)
        turned = jnp.transpose(taps).astype(BF16)
        for b in range(3):
            wf[b * chip + core * own : b * chip + (core + 1) * own, :] = turned[b * own : (b + 1) * own]
        narrow = taps.astype(BF16)
        for a in range(3):
            for b in range(3):
                goal = (2 - a) * chip + core * own
                for part in range(2):
                    base = pl.multiple_of(b * every + chip * jnp.where(l == part, 0, 1), 16)
                    start = a * every + part * chip
                    wb[pl.ds(base, chip), goal : goal + own] = narrow[
                        start : start + chip, b * own : (b + 1) * own
                    ]

    load_x.wait()
    load_g.wait()
    for which, ref in ((0, mine(xs, 1 - c, rows + 1, sib)), (1, mine(gs, 0, rows, 1 - c))):
        remote(ref, ref, bsend.at[which], brecv.at[which], chan=sib).wait_recv()
    def border():
        at = pl.ds(pl.multiple_of(own * other, 16), chip)
        return remote(
            xs.at[jnp.where(c == 0, rows, 1), at], xs.at[jnp.where(c == 0, 0, rows + 1), at],
            bsend.at[3], brecv.at[3], chan=sib,
        )

    def await_rows(s, start, n):
        for of in range(2):
            ref = mine(xs, start, n, other + of)
            remote(ref, ref, isend.at[of, s], irecv.at[of, s], chan=other + of).wait_recv()

    place = 2 * row + c

    def down_copy():
        return remote(ss.at[rows], ss.at[0], ssend.at[0], srecv.at[0], row=row + c, chan=sib)

    def up_copy():
        return remote(ss.at[1], ss.at[rows + 1], ssend.at[1], srecv.at[1], row=row - (1 - c), chan=sib)

    def trade():
        return remote(acc.at[1 - c], kin, ksend.at[0, 0], krecv.at[0, 0], chan=sib)

    def plane_copies():
        made = []
        for k in range(1, side):
            f, to = on_first(k)
            made.append(remote(kp.at[f], kr.at[k], ksend.at[1, k], krecv.at[1, k], dp=to))
        return made

    def act_copies(k):
        at = pl.ds(k * ROWS, ROWS)
        to = pl.ds(rows * c + k * ROWS, ROWS)
        return (
            pltpu.make_async_copy(ab.at[c, at], act_out.at[to], alocal.at[k]),
            remote(ab.at[1 - c, at], act_out.at[to], asend.at[k], arecv.at[k], chan=sib),
        )

    def near_copies(k):
        at = pl.ds(k * ROWS, ROWS)
        to = pl.ds(rows * c + k * ROWS, ROWS)
        return (
            pltpu.make_async_copy(pf.at[c, at], grad_out.at[to], plocal.at[k]),
            remote(pf.at[1 - c, at], grad_out.at[to], psend.at[k], precv.at[k], chan=sib),
        )

    def far_copies(k):
        at = pl.ds(k * ROWS, ROWS)
        to = pl.ds(rows * c + k * ROWS, ROWS)
        return (
            remote(pb.at[0, at], arrived.at[to], csend.at[0, k], crecv.at[c, k], chan=other),
            remote(pb.at[1, at], arrived.at[to], csend.at[1, k], crecv.at[c, k], chan=other + 1),
        )

    def chunk_at(s):
        return jnp.where(s < 2, jnp.where(s == c, chunks - 1, 0), s - 1)

    def three(ref, start):
        block = ref[pl.ds(start, 3)]
        return block.reshape(3 * ref.shape[1], width)

    def forward(k):
        for pair in range(ROWS // 2):
            q = k * ROWS + 2 * pair
            right = jnp.concatenate([three(xs, q), three(xs, q + 1)], axis=1)
            taps = jnp.dot(wf[...], right, preferred_element_type=F32)
            for u in range(2):
                at = slice(u * width, (u + 1) * width)
                pre = shift_right(taps[0:chip, at]) + taps[chip : 2 * chip, at] + shift_left(taps[2 * chip :, at])
                sigma = 1.0 / (1.0 + jnp.exp(-pre))
                done = (pre * sigma).astype(BF16)
                for core in range(2):
                    ab[core, q + u] = done[core * own : (core + 1) * own]
                slope = gs[q + u].astype(F32) * sigma * (1.0 + pre * (1.0 - sigma))
                slope = slope.astype(BF16)
                ss[q + u + 1] = slope
                wide_slope = slope.astype(F32)
                turned = (shift_left(wide_slope).astype(BF16), slope, shift_right(wide_slope).astype(BF16))
                to = slice((2 * pair + u) * width, (2 * pair + u + 1) * width)
                for core in range(2):
                    for b in range(3):
                        s3[k, core * lanes + b * own : core * lanes + (b + 1) * own, to] = turned[b][
                            core * own : (core + 1) * own
                        ]

    def kernel_terms(k):
        left = jnp.concatenate([three(xs, k * ROWS + u) for u in range(ROWS)], axis=1)
        term = lax.dot_general(left, s3[k], (((1,), (1,)), ((), ())), preferred_element_type=F32)
        for core in range(2):
            acc[core] += term[:, core * lanes : (core + 1) * lanes]

    def backward(k):
        for pair in range(ROWS // 2):
            q = k * ROWS + 2 * pair
            right = jnp.concatenate([three(ss, q), three(ss, q + 1)], axis=1)
            taps = jnp.dot(wb[...], right, preferred_element_type=F32)
            for u in range(2):
                at = slice(u * width, (u + 1) * width)
                grad = (
                    shift_left(taps[0:every, at])
                    + taps[every : 2 * every, at]
                    + shift_right(taps[2 * every :, at])
                )
                for core in range(2):
                    pf[core, q + u] = grad[core * own : (core + 1) * own]
                    pb[core, q + u] = grad[chip + core * own : chip + (core + 1) * own].astype(BF16)

    @pl.loop(0, chunks + 3)
    def _(s):
        @pl.when(s < 2)
        def _():
            piece = jnp.where(s == 0, c, 1 - c)
            await_rows(piece, jnp.where(piece == 0, rows - ROWS, 1), ROWS + 1)

        @pl.when(s == 0)
        def _():
            border().start()
            border().wait_recv()

        @pl.when(jnp.logical_and(s == 1, c != row))
        def _():
            for g in range(4):
                ref = mine(xs, (rows + 1) * c, 1, g)
                remote(ref, ref, hsend.at[0], hrecv.at[g], row=1 - row, chan=g).wait_recv()

        @pl.when(s == chunks - 1)
        def _():
            await_rows(chunks - 1, *pieces[chunks - 1])

        @pl.when(jnp.logical_and(s > 1, s < chunks - 1))
        def _():
            await_rows(s, ROWS * (s - 1) + 2, ROWS)

        @pl.when(s < chunks)
        def _():
            k = chunk_at(s)
            forward(k)
            for copy in act_copies(k):
                copy.start()

        @pl.when(jnp.logical_and(s > chunks // 2, s < chunks))
        def _():
            kernel_terms(chunk_at(2 * (s - chunks // 2) - 2))
            kernel_terms(chunk_at(2 * (s - chunks // 2) - 1))

        @pl.when(s == chunks - 1)
        def _():
            for t in range(2 * (chunks - 1 - chunks // 2), chunks):
                kernel_terms(chunk_at(t))

        @pl.when(jnp.logical_and(s == c, place < 3))
        def _():
            down_copy().start()

        @pl.when(jnp.logical_and(s == 1 - c, place > 0))
        def _():
            up_copy().start()

        @pl.when(s == chunks - 1)
        def _():
            trade().start()

        @pl.when(jnp.logical_and(s == chunks + 1, place < 3))
        def _():
            up_copy().wait_recv()

        @pl.when(jnp.logical_and(s == chunks + 2, place > 0))
        def _():
            down_copy().wait_recv()

        @pl.when(s >= 3)
        def _():
            k = lax.rem(s - 2, chunks)
            backward(k)
            for copy in near_copies(k):
                copy.start()

            @pl.when(s < chunks + 3 - HELD)
            def _():
                for copy in far_copies(k):
                    copy.start()

        @pl.when(s == chunks - 1)
        def _():
            trade().wait()
            kin[...] += acc[c]
            for i in range(side):
                for j in range(side):
                    f = jnp.where(c == 0, j, i)
                    to = jnp.where(c == 0, i, j)
                    d = i * side + j
                    for a in range(3):
                        kp[f, to, a * share : (a + 1) * share, :] = kin[
                            a * every + d * share : a * every + (d + 1) * share, :
                        ]
            for copy in plane_copies():
                copy.start()

    for copy in plane_copies():
        copy.wait()
    total = kp[first]
    for k in range(1, side):
        total += kr[k]
    ksum[...] = total
    copies = []
    for k in range(1, side):
        s, to = on_second(k)
        copy = remote(ksum.at[s], kr2.at[k], ksend.at[2, k], krecv.at[2, k], dp=to)
        copy.start()
        copies.append(copy)
    for copy in copies:
        copy.wait()
    total = ksum[second]
    for k in range(1, side):
        total += kr2[k]
    kt[...] = total
    copy = remote(kt, kq, ksend.at[3, 0], krecv.at[3, 0], row=1 - row)
    copy.start()
    for s in range(chunks + 3 - HELD, chunks + 3):
        for far in far_copies((s - 2) % chunks):
            far.start()
    copy.wait()
    kg_out[...] = kt[...] + kq[...]

    @pl.loop(1, chunks + 1)
    def _(k):
        k = lax.rem(k, chunks)
        for copy in near_copies(k):
            copy.wait()
        for of in range(2):
            at = pl.ds(rows * of + k * ROWS, ROWS)
            ref = arrived.at[at]
            remote(ref, ref, csend.at[of, k], crecv.at[of, k], chan=other + of).wait_recv()
            grad_out[at] += arrived[at].astype(F32)

    for copy in sent:
        copy.wait_send()
    border().wait_send()

    @pl.when(place < 3)
    def _():
        down_copy().wait_send()

    @pl.when(place > 0)
    def _():
        up_copy().wait_send()

    @pl.loop(0, chunks)
    def _(k):
        for copy in act_copies(k):
            copy.wait()
        for copy in far_copies(k):
            copy.wait_send()


def finish(own, share, act, grad, terms, act_out, grad_out, kg_out, kg, sems):
    step = grad.shape[0] // PARTS
    copies = []
    for p in range(PARTS):
        at = pl.ds(p * step, step)
        copies.append(pltpu.make_async_copy(grad.at[at], grad_out.at[at], sems.at[p, 0]))
        copies.append(pltpu.make_async_copy(act.at[at], act_out.at[at], sems.at[p, 1]))
    for copy in copies:
        copy.start()
    for a in range(3):
        for b in range(3):
            kg[3 * a + b] = terms[a * share : (a + 1) * share, b * own : (b + 1) * own]
    last = pltpu.make_async_copy(kg, kg_out, sems.at[PARTS, 0])
    last.start()
    for copy in copies:
        copy.wait()
    last.wait()


def shards(images, kernel, cotangent):
    _, height, own, width = images.shape
    share = kernel.shape[1]
    side = math.isqrt(lax.axis_size("dp"))
    rows = height // 2
    chunks = rows // ROWS
    chip, every = 2 * own, 4 * own
    pad_share = round_up(3 * share, 16)
    lanes = round_up(3 * own, 128)
    dma = pltpu.SemaphoreType.DMA
    scratch = [
        pltpu.VMEM((rows + 2, every, width), BF16),
        pltpu.VMEM((rows, chip, width), BF16),
        pltpu.VMEM((rows + 2, chip, width), BF16),
        pltpu.VMEM((chunks, 2 * lanes, ROWS * width), BF16),
        pltpu.VMEM((2, 3 * every, lanes), F32),
        pltpu.VMEM(kernel.shape, BF16),
        pltpu.VMEM((pad_share, lanes), F32),
        pltpu.VMEM((2, side, side, pad_share, lanes), BF16),
        pltpu.VMEM((3 * every, side * side * pad_share), BF16),
        pltpu.VMEM((3 * chip, 3 * every), BF16),
        pltpu.VMEM((3 * every, 3 * chip), BF16),
        pltpu.VMEM((2, rows, own, width), BF16),
        pltpu.VMEM((2, rows, own, width), F32),
        pltpu.VMEM((2, rows, own, width), BF16),
        pltpu.VMEM((height, own, width), BF16),
        pltpu.VMEM((3 * every, lanes), F32),
        pltpu.VMEM((side, side, pad_share, lanes), F32),
        pltpu.VMEM((side, side, pad_share, lanes), F32),
        pltpu.VMEM((side, pad_share, lanes), F32),
        pltpu.VMEM((side, pad_share, lanes), F32),
        pltpu.VMEM((pad_share, lanes), F32),
        pltpu.VMEM((pad_share, lanes), F32),
        dma((3,)),
        dma((2, side)), dma((2, side)),
        dma((2, chunks)), dma((2, chunks)),
        dma((2,)), dma((4,)),
        dma((4,)), dma((4,)),
        dma((2,)), dma((2,)),
        dma((chunks,)), dma((chunks,)), dma((chunks,)),
        dma((chunks,)), dma((chunks,)), dma((chunks,)),
        dma((2, chunks)), dma((2, chunks)),
        dma((4, side)), dma((4, side)),
        dma((side,)), dma((side,)),
        pltpu.SemaphoreType.REGULAR, pltpu.SemaphoreType.REGULAR,
    ]
    hbm = pl.BlockSpec(memory_space=pl.ANY)
    vmem = pl.BlockSpec(memory_space=pltpu.VMEM)
    activated, input_grad, terms = pl.pallas_call(
        functools.partial(body, side, own, share, height, width),
        out_shape=(
            pltpu.VMEM((height, own, width), BF16),
            pltpu.VMEM((height, own, width), F32),
            pltpu.VMEM((pad_share, lanes), F32),
        ),
        in_specs=[hbm] * 3,
        out_specs=(vmem,) * 3,
        scratch_shapes=scratch,
        compiler_params=pltpu.CompilerParams(
            collective_id=0, has_side_effects=True, vmem_limit_bytes=56 * 2**20
        ),
        name="conv_block",
    )(images[0], kernel, cotangent[0])
    activated, input_grad, kernel_grad = pl.pallas_call(
        functools.partial(finish, own, share),
        out_shape=(
            jax.ShapeDtypeStruct((height, own, width), BF16),
            jax.ShapeDtypeStruct((height, own, width), F32),
            jax.ShapeDtypeStruct((9, share, own), F32),
        ),
        in_specs=[vmem] * 3,
        out_specs=(hbm, hbm, hbm),
        scratch_shapes=[pltpu.VMEM((9, share, own), F32), dma((PARTS + 1, 2))],
        compiler_params=pltpu.CompilerParams(vmem_limit_bytes=16 * 2**20),
        name="results",
    )(activated, input_grad, terms)
    return activated[None], input_grad[None], kernel_grad


def solution(mesh):
    placed = (P("dp", "row", "chan", None), P(None, "dp", "chan"), P("dp", "row", "chan", None))
    return jax.shard_map(
        shards,
        mesh=mesh,
        in_specs=placed,
        out_specs=(
            P("dp", "row", "chan", None),
            P("dp", "row", "chan", None),
            P(None, "dp", "chan"),
        ),
        check_vma=False,
    )
```

```python
import functools
import math

import jax
import jax.numpy as jnp
from jax import lax
from jax.experimental import pallas as pl
from jax.experimental.pallas import tpu as pltpu
from jax.sharding import PartitionSpec as P

MESH = pl.DeviceIdType.MESH
BF16 = jnp.bfloat16
F32 = jnp.float32
ROWS = 4
PARTS = 4
LAG = 4
HELD = 1


def round_up(x, m):
    return (x + m - 1) // m * m


def remote(src, dst, send, recv, **where):
    return pltpu.make_async_remote_copy(
        src_ref=src, dst_ref=dst, send_sem=send, recv_sem=recv, device_id=where, device_id_type=MESH
    )


def shift_right(x):
    lane = lax.broadcasted_iota(jnp.int32, x.shape, 1)
    return jnp.where(lane == 0, 0.0, pltpu.roll(x, 1, 1))


def shift_left(x):
    lane = lax.broadcasted_iota(jnp.int32, x.shape, 1)
    return jnp.where(lane == x.shape[1] - 1, 0.0, pltpu.roll(x, x.shape[1] - 1, 1))


def body(
    side, own, share, height, width,
    img, ker, cot,
    act_out, grad_out, kg_out,
    xs, gs, ss, s3, acc, wk, wpk, wraw, em, wf, wb, ab, pf, pb,
    arrived, kin, kp, kr, ksum, kr2, kt, kq,
    local, wsend, wrecv, isend, irecv, hsend, hrecv, bsend, brecv,
    ssend, srecv, asend, arecv, alocal, plocal, psend, precv, csend, crecv, ksend, krecv,
    fsend, frecv, near_ready, plane_ready, slab_ready,
):
    rows = height // 2
    chunks = rows // ROWS
    chip = 2 * own
    every = 4 * own
    pad_share = wpk.shape[0]
    lanes = s3.shape[1] // 2

    dp = lax.axis_index("dp")
    chan = lax.axis_index("chan")
    row = lax.axis_index("row")
    l = chan // 2
    c = lax.rem(chan, 2)
    sib = 2 * l + 1 - c
    other = 2 * (1 - l)
    y = dp // side
    x = lax.rem(dp, side)
    first = jnp.where(c == 0, x, y)
    second = jnp.where(c == 0, y, x)
    step_first = jnp.where(c == 0, 1, side)
    step_second = jnp.where(c == 0, side, 1)

    def on_first(k):
        f = lax.rem(first + k, side)
        return f, f * step_first + second * step_second

    def on_second(k):
        s = lax.rem(second + k, side)
        return s, first * step_first + s * step_second

    barrier = pltpu.get_barrier_semaphore()

    def tell(sem, **where):
        pl.semaphore_signal(sem, inc=1, device_id=where, device_id_type=MESH)

    tell(barrier, chan=other + 1)

    @pl.when(c == 0)
    def _():
        tell(barrier, chan=sib)

    for k in range(1, side):
        for to in (on_first(k)[1], on_second(k)[1]):
            tell(barrier, dp=to, chan=0)
    tell(barrier, row=1 - row, chan=2)

    def agree(teller, number, sem):
        @pl.when(chan == teller)
        def _():
            pl.semaphore_wait(barrier, number)
            for k in range(1, 4):
                tell(sem, chan=(teller + k) % 4)

        @pl.when(chan != teller)
        def _():
            pl.semaphore_wait(sem, 1)

    def mine(ref, first_row, n, g):
        return ref.at[pl.ds(first_row, n), pl.ds(pl.multiple_of(own * g, 16), own)]

    load_k = pltpu.make_async_copy(ker, wk, local.at[0])
    load_k.start()
    load_x = pltpu.make_async_copy(
        img.at[pl.ds((rows - 1) * c, rows + 1)], mine(xs, 1 - c, rows + 1, chan), local.at[1]
    )
    load_x.start()
    load_g = pltpu.make_async_copy(cot.at[pl.ds(rows * c, rows)], mine(gs, 0, rows, c), local.at[2])
    load_g.start()

    @pl.when(c == 1)
    def _():
        pl.semaphore_wait(barrier, 3)
        tell(near_ready, chan=sib)

    @pl.when(c == 0)
    def _():
        pl.semaphore_wait(near_ready, 1)

    pieces = [(rows - ROWS, ROWS + 1), (1, ROWS + 1)]
    pieces += [(ROWS * k + 2, ROWS) for k in range(1, chunks - 2)]
    pieces += [(ROWS * (chunks - 2) + 2, ROWS - 2)]
    sent = []

    def send(*args, **where):
        copy = remote(*args, **where)
        copy.start()
        sent.append(copy)

    def send_piece(to, s):
        start, n = pieces[s]
        send(
            img.at[pl.ds(rows * to + start - 1, n)], mine(xs, start, n, chan),
            isend.at[to, s], irecv.at[c, s], chan=other + to,
        )

    send_piece(0, 0)
    send_piece(1, 1)
    send(
        img.at[pl.ds((rows - 1) * (1 - c), rows + 1)], mine(xs, c, rows + 1, chan),
        bsend.at[0], brecv.at[0], chan=sib,
    )
    send(cot.at[pl.ds(rows * (1 - c), rows)], mine(gs, 0, rows, c), bsend.at[1], brecv.at[1], chan=sib)
    send_piece(0, 1)
    send_piece(1, 0)
    for to in range(2):
        send_piece(to, 2)

    wpk[...] = jnp.zeros_like(wpk)
    load_k.wait()
    for b in range(3):
        for a in range(3):
            wpk[a * share : (a + 1) * share, b * own : (b + 1) * own] = wk[3 * a + b].astype(F32)
    wraw[c, second, first] = wpk[...].astype(BF16)

    agree(0, 8 * (side - 1), plane_ready)

    gather = []
    for k in range(1, side):
        spot = wraw.at[c, second, first]
        copy = remote(spot, spot, wsend.at[0, k], wrecv.at[0, k], dp=on_first(k)[1])
        copy.start()
        gather.append(copy)

    for core in range(2):
        s3[:, core * lanes + 3 * own : (core + 1) * lanes, :] = jnp.zeros((chunks, lanes - 3 * own, s3.shape[2]), BF16)

    @pl.when(jnp.logical_and(c == 0, row == 0))
    def _():
        xs[0] = jnp.zeros(xs.shape[1:], BF16)
        ss[0] = jnp.zeros(ss.shape[1:], BF16)

    @pl.when(jnp.logical_and(c == 1, row == 1))
    def _():
        xs[rows + 1] = jnp.zeros(xs.shape[1:], BF16)
        ss[rows + 1] = jnp.zeros(ss.shape[1:], BF16)

    acc[...] = jnp.zeros_like(acc)
    spot = lax.broadcasted_iota(jnp.int32, (1, em.shape[1]), 1)
    owner = jnp.zeros_like(spot)
    for k in range(1, side * side):
        owner += (spot >= k * pad_share).astype(jnp.int32)
    within = spot - owner * pad_share
    tap = (within >= share).astype(jnp.int32) + (within >= 2 * share).astype(jnp.int32)
    target = tap * every + owner * share + within - tap * share
    target = jnp.where(within < 3 * share, target, -1)
    em[...] = (lax.broadcasted_iota(jnp.int32, em.shape, 0) == target).astype(F32).astype(BF16)

    agree(2, 4, slab_ready)
    for to in range(2):
        send(
            img.at[pl.ds((height - 1) * (1 - row), 1)], mine(xs, (rows + 1) * row, 1, chan),
            hsend.at[to], hrecv.at[chan], row=1 - row, chan=2 * to + row,
        )
    for s in range(3, chunks):
        for to in range(2):
            send_piece(to, s)

    for copy in gather:
        copy.wait()
    spot = wraw.at[c, second]
    gather = [remote(spot, spot, wsend.at[1, k], wrecv.at[1, k], dp=on_second(k)[1]) for k in range(1, side)]
    for copy in gather:
        copy.start()
    send(spot, spot, fsend.at[0], frecv.at[0], chan=sib)
    for k in range(1, side):
        gather[k - 1].wait()
        spot = wraw.at[c, lax.rem(second + side - k, side)]
        send(spot, spot, fsend.at[k], frecv.at[k], chan=sib)
    for k in range(side):
        spot = wraw.at[1 - c, k]
        remote(spot, spot, fsend.at[k], frecv.at[k], chan=sib).wait_recv()

    for core in range(2):
        order = [(i, j) if core == 0 else (j, i) for i in range(side) for j in range(side)]
        blocks = jnp.concatenate([wraw[core, i, j] for i, j in order], axis=0)
        taps = jnp.dot(em[...], blocks, preferred_element_type=F32)
        turned = jnp.transpose(taps).astype(BF16)
        for b in range(3):
            wf[b * chip + core * own : b * chip + (core + 1) * own, :] = turned[b * own : (b + 1) * own]
        narrow = taps.astype(BF16)
        for a in range(3):
            for b in range(3):
                goal = (2 - a) * chip + core * own
                for part in range(2):
                    base = pl.multiple_of(b * every + chip * jnp.where(l == part, 0, 1), 16)
                    start = a * every + part * chip
                    wb[pl.ds(base, chip), goal : goal + own] = narrow[
                        start : start + chip, b * own : (b + 1) * own
                    ]

    load_x.wait()
    load_g.wait()
    for which, ref in ((0, mine(xs, 1 - c, rows + 1, sib)), (1, mine(gs, 0, rows, 1 - c))):
        remote(ref, ref, bsend.at[which], brecv.at[which], chan=sib).wait_recv()
    def border():
        at = pl.ds(pl.multiple_of(own * other, 16), chip)
        return remote(
            xs.at[jnp.where(c == 0, rows, 1), at], xs.at[jnp.where(c == 0, 0, rows + 1), at],
            bsend.at[3], brecv.at[3], chan=sib,
        )

    def await_rows(s, start, n):
        for of in range(2):
            ref = mine(xs, start, n, other + of)
            remote(ref, ref, isend.at[of, s], irecv.at[of, s], chan=other + of).wait_recv()

    place = 2 * row + c

    def down_copy():
        return remote(ss.at[rows], ss.at[0], ssend.at[0], srecv.at[0], row=row + c, chan=sib)

    def up_copy():
        return remote(ss.at[1], ss.at[rows + 1], ssend.at[1], srecv.at[1], row=row - (1 - c), chan=sib)

    def trade():
        return remote(acc.at[1 - c], kin, ksend.at[0, 0], krecv.at[0, 0], chan=sib)

    def plane_copies():
        made = []
        for k in range(1, side):
            f, to = on_first(k)
            made.append(remote(kp.at[f], kr.at[k], ksend.at[1, k], krecv.at[1, k], dp=to))
        return made

    def act_copies(k):
        at = pl.ds(k * ROWS, ROWS)
        to = pl.ds(rows * c + k * ROWS, ROWS)
        return (
            pltpu.make_async_copy(ab.at[c, at], act_out.at[to], alocal.at[k]),
            remote(ab.at[1 - c, at], act_out.at[to], asend.at[k], arecv.at[k], chan=sib),
        )

    def near_copies(k):
        at = pl.ds(k * ROWS, ROWS)
        to = pl.ds(rows * c + k * ROWS, ROWS)
        return (
            pltpu.make_async_copy(pf.at[c, at], grad_out.at[to], plocal.at[k]),
            remote(pf.at[1 - c, at], grad_out.at[to], psend.at[k], precv.at[k], chan=sib),
        )

    def far_copies(k):
        at = pl.ds(k * ROWS, ROWS)
        to = pl.ds(rows * c + k * ROWS, ROWS)
        return (
            remote(pb.at[0, at], arrived.at[to], csend.at[0, k], crecv.at[c, k], chan=other),
            remote(pb.at[1, at], arrived.at[to], csend.at[1, k], crecv.at[c, k], chan=other + 1),
        )

    def chunk_at(s):
        return jnp.where(s < 2, jnp.where(s == c, chunks - 1, 0), s - 1)

    def three(ref, start):
        block = ref[pl.ds(start, 3)]
        return block.reshape(3 * ref.shape[1], width)

    def forward(k):
        for pair in range(ROWS // 2):
            q = k * ROWS + 2 * pair
            right = jnp.concatenate([three(xs, q), three(xs, q + 1)], axis=1)
            taps = jnp.dot(wf[...], right, preferred_element_type=F32)
            for u in range(2):
                at = slice(u * width, (u + 1) * width)
                pre = shift_right(taps[0:chip, at]) + taps[chip : 2 * chip, at] + shift_left(taps[2 * chip :, at])
                sigma = 1.0 / (1.0 + jnp.exp(-pre))
                done = (pre * sigma).astype(BF16)
                for core in range(2):
                    ab[core, q + u] = done[core * own : (core + 1) * own]
                slope = gs[q + u].astype(F32) * sigma * (1.0 + pre * (1.0 - sigma))
                slope = slope.astype(BF16)
                ss[q + u + 1] = slope
                wide_slope = slope.astype(F32)
                turned = (shift_left(wide_slope).astype(BF16), slope, shift_right(wide_slope).astype(BF16))
                to = slice((2 * pair + u) * width, (2 * pair + u + 1) * width)
                for core in range(2):
                    for b in range(3):
                        s3[k, core * lanes + b * own : core * lanes + (b + 1) * own, to] = turned[b][
                            core * own : (core + 1) * own
                        ]

    def kernel_terms(k):
        left = jnp.concatenate([three(xs, k * ROWS + u) for u in range(ROWS)], axis=1)
        term = lax.dot_general(left, s3[k], (((1,), (1,)), ((), ())), preferred_element_type=F32)
        for core in range(2):
            acc[core] += term[:, core * lanes : (core + 1) * lanes]

    def backward(k):
        for pair in range(ROWS // 2):
            q = k * ROWS + 2 * pair
            right = jnp.concatenate([three(ss, q), three(ss, q + 1)], axis=1)
            taps = jnp.dot(wb[...], right, preferred_element_type=F32)
            for u in range(2):
                at = slice(u * width, (u + 1) * width)
                grad = (
                    shift_left(taps[0:every, at])
                    + taps[every : 2 * every, at]
                    + shift_right(taps[2 * every :, at])
                )
                for core in range(2):
                    pf[core, q + u] = grad[core * own : (core + 1) * own]
                    pb[core, q + u] = grad[chip + core * own : chip + (core + 1) * own].astype(BF16)

    steps = chunks + LAG

    @pl.loop(0, steps)
    def _(s):
        @pl.when(s < 2)
        def _():
            piece = jnp.where(s == 0, c, 1 - c)
            await_rows(piece, jnp.where(piece == 0, rows - ROWS, 1), ROWS + 1)

        @pl.when(s == 0)
        def _():
            border().start()
            border().wait_recv()

        @pl.when(jnp.logical_and(s == 1, c != row))
        def _():
            for g in range(4):
                ref = mine(xs, (rows + 1) * c, 1, g)
                remote(ref, ref, hsend.at[0], hrecv.at[g], row=1 - row, chan=g).wait_recv()

        @pl.when(s == chunks - 1)
        def _():
            await_rows(chunks - 1, *pieces[chunks - 1])

        @pl.when(jnp.logical_and(s > 1, s < chunks - 1))
        def _():
            await_rows(s, ROWS * (s - 1) + 2, ROWS)

        @pl.when(s < chunks)
        def _():
            k = chunk_at(s)
            forward(k)
            for copy in act_copies(k):
                copy.start()

        @pl.when(jnp.logical_and(s >= chunks // 2, s < chunks))
        def _():
            kernel_terms(chunk_at(2 * s - chunks + 1))

        @pl.when(jnp.logical_and(s >= chunks // 2 - 1, s < chunks - 1))
        def _():
            kernel_terms(chunk_at(2 * s - chunks + 2))

        @pl.when(jnp.logical_and(s == c, place < 3))
        def _():
            down_copy().start()

        @pl.when(jnp.logical_and(s == 1 - c, place > 0))
        def _():
            up_copy().start()

        @pl.when(s == chunks - 1)
        def _():
            trade().start()

        @pl.when(jnp.logical_and(s == steps - 2, place < 3))
        def _():
            up_copy().wait_recv()

        @pl.when(jnp.logical_and(s == steps - 1, place > 0))
        def _():
            down_copy().wait_recv()

        @pl.when(s >= LAG)
        def _():
            k = lax.rem(s - LAG + 1, chunks)
            backward(k)
            for copy in near_copies(k):
                copy.start()

            @pl.when(s < steps - HELD)
            def _():
                for copy in far_copies(k):
                    copy.start()

        @pl.when(s == chunks - 1)
        def _():
            trade().wait()
            kin[...] += acc[c]
            for i in range(side):
                for j in range(side):
                    f = jnp.where(c == 0, j, i)
                    to = jnp.where(c == 0, i, j)
                    d = i * side + j
                    for a in range(3):
                        kp[f, to, a * share : (a + 1) * share, :] = kin[
                            a * every + d * share : a * every + (d + 1) * share, :
                        ]
            for copy in plane_copies():
                copy.start()

    for copy in plane_copies():
        copy.wait()
    total = kp[first]
    for k in range(1, side):
        total += kr[k]
    ksum[...] = total
    copies = []
    for k in range(1, side):
        s, to = on_second(k)
        copy = remote(ksum.at[s], kr2.at[k], ksend.at[2, k], krecv.at[2, k], dp=to)
        copy.start()
        copies.append(copy)
    for copy in copies:
        copy.wait()
    total = ksum[second]
    for k in range(1, side):
        total += kr2[k]
    kt[...] = total.astype(BF16)
    copy = remote(kt, kq, ksend.at[3, 0], krecv.at[3, 0], row=1 - row)
    copy.start()
    for s in range(steps - HELD, steps):
        for far in far_copies((s - LAG + 1) % chunks):
            far.start()
    copy.wait()
    kg_out[...] = kt[...].astype(F32) + kq[...].astype(F32)

    @pl.loop(1, chunks + 1)
    def _(k):
        k = lax.rem(k, chunks)
        for copy in near_copies(k):
            copy.wait()
        for of in range(2):
            at = pl.ds(rows * of + k * ROWS, ROWS)
            ref = arrived.at[at]
            remote(ref, ref, csend.at[of, k], crecv.at[of, k], chan=other + of).wait_recv()
            grad_out[at] += arrived[at].astype(F32)

    for copy in sent:
        copy.wait_send()
    border().wait_send()

    @pl.when(place < 3)
    def _():
        down_copy().wait_send()

    @pl.when(place > 0)
    def _():
        up_copy().wait_send()

    @pl.loop(0, chunks)
    def _(k):
        for copy in act_copies(k):
            copy.wait()
        for copy in far_copies(k):
            copy.wait_send()


def finish(own, share, act, grad, terms, act_out, grad_out, kg_out, kg, sems):
    step = grad.shape[0] // PARTS
    copies = []
    for p in range(PARTS):
        at = pl.ds(p * step, step)
        copies.append(pltpu.make_async_copy(grad.at[at], grad_out.at[at], sems.at[p, 0]))
        copies.append(pltpu.make_async_copy(act.at[at], act_out.at[at], sems.at[p, 1]))
    for copy in copies:
        copy.start()
    for a in range(3):
        for b in range(3):
            kg[3 * a + b] = terms[a * share : (a + 1) * share, b * own : (b + 1) * own]
    last = pltpu.make_async_copy(kg, kg_out, sems.at[PARTS, 0])
    last.start()
    for copy in copies:
        copy.wait()
    last.wait()


def shards(images, kernel, cotangent):
    _, height, own, width = images.shape
    share = kernel.shape[1]
    side = math.isqrt(lax.axis_size("dp"))
    rows = height // 2
    chunks = rows // ROWS
    chip, every = 2 * own, 4 * own
    pad_share = round_up(3 * share, 16)
    lanes = round_up(3 * own, 128)
    dma = pltpu.SemaphoreType.DMA
    scratch = [
        pltpu.VMEM((rows + 2, every, width), BF16),
        pltpu.VMEM((rows, chip, width), BF16),
        pltpu.VMEM((rows + 2, chip, width), BF16),
        pltpu.VMEM((chunks, 2 * lanes, ROWS * width), BF16),
        pltpu.VMEM((2, 3 * every, lanes), F32),
        pltpu.VMEM(kernel.shape, BF16),
        pltpu.VMEM((pad_share, lanes), F32),
        pltpu.VMEM((2, side, side, pad_share, lanes), BF16),
        pltpu.VMEM((3 * every, side * side * pad_share), BF16),
        pltpu.VMEM((3 * chip, 3 * every), BF16),
        pltpu.VMEM((3 * every, 3 * chip), BF16),
        pltpu.VMEM((2, rows, own, width), BF16),
        pltpu.VMEM((2, rows, own, width), F32),
        pltpu.VMEM((2, rows, own, width), BF16),
        pltpu.VMEM((height, own, width), BF16),
        pltpu.VMEM((3 * every, lanes), F32),
        pltpu.VMEM((side, side, pad_share, lanes), F32),
        pltpu.VMEM((side, side, pad_share, lanes), F32),
        pltpu.VMEM((side, pad_share, lanes), F32),
        pltpu.VMEM((side, pad_share, lanes), F32),
        pltpu.VMEM((pad_share, lanes), BF16),
        pltpu.VMEM((pad_share, lanes), BF16),
        dma((3,)),
        dma((2, side)), dma((2, side)),
        dma((2, chunks)), dma((2, chunks)),
        dma((2,)), dma((4,)),
        dma((4,)), dma((4,)),
        dma((2,)), dma((2,)),
        dma((chunks,)), dma((chunks,)), dma((chunks,)),
        dma((chunks,)), dma((chunks,)), dma((chunks,)),
        dma((2, chunks)), dma((2, chunks)),
        dma((4, side)), dma((4, side)),
        dma((side,)), dma((side,)),
        pltpu.SemaphoreType.REGULAR, pltpu.SemaphoreType.REGULAR, pltpu.SemaphoreType.REGULAR,
    ]
    hbm = pl.BlockSpec(memory_space=pl.ANY)
    vmem = pl.BlockSpec(memory_space=pltpu.VMEM)
    activated, input_grad, terms = pl.pallas_call(
        functools.partial(body, side, own, share, height, width),
        out_shape=(
            pltpu.VMEM((height, own, width), BF16),
            pltpu.VMEM((height, own, width), F32),
            pltpu.VMEM((pad_share, lanes), F32),
        ),
        in_specs=[hbm] * 3,
        out_specs=(vmem,) * 3,
        scratch_shapes=scratch,
        compiler_params=pltpu.CompilerParams(
            collective_id=0, has_side_effects=True, vmem_limit_bytes=56 * 2**20
        ),
        name="conv_block",
    )(images[0], kernel, cotangent[0])
    activated, input_grad, kernel_grad = pl.pallas_call(
        functools.partial(finish, own, share),
        out_shape=(
            jax.ShapeDtypeStruct((height, own, width), BF16),
            jax.ShapeDtypeStruct((height, own, width), F32),
            jax.ShapeDtypeStruct((9, share, own), F32),
        ),
        in_specs=[vmem] * 3,
        out_specs=(hbm, hbm, hbm),
        scratch_shapes=[pltpu.VMEM((9, share, own), F32), dma((PARTS + 1, 2))],
        compiler_params=pltpu.CompilerParams(vmem_limit_bytes=16 * 2**20),
        name="results",
    )(activated, input_grad, terms)
    return activated[None], input_grad[None], kernel_grad


def solution(mesh):
    placed = (P("dp", "row", "chan", None), P(None, "dp", "chan"), P("dp", "row", "chan", None))
    return jax.shard_map(
        shards,
        mesh=mesh,
        in_specs=placed,
        out_specs=(
            P("dp", "row", "chan", None),
            P("dp", "row", "chan", None),
            P(None, "dp", "chan"),
        ),
        check_vma=False,
    )
```

```python
import functools
import math

import jax
import jax.numpy as jnp
from jax import lax
from jax.experimental import pallas as pl
from jax.experimental.pallas import tpu as pltpu
from jax.sharding import PartitionSpec as P

MESH = pl.DeviceIdType.MESH
BF16 = jnp.bfloat16
F32 = jnp.float32
ROWS = 4
PARTS = 4
LAG = 4
HELD = 1


def round_up(x, m):
    return (x + m - 1) // m * m


def remote(src, dst, send, recv, **where):
    return pltpu.make_async_remote_copy(
        src_ref=src, dst_ref=dst, send_sem=send, recv_sem=recv, device_id=where, device_id_type=MESH
    )


def shift_right(x):
    lane = lax.broadcasted_iota(jnp.int32, x.shape, 1)
    return jnp.where(lane == 0, 0.0, pltpu.roll(x, 1, 1))


def shift_left(x):
    lane = lax.broadcasted_iota(jnp.int32, x.shape, 1)
    return jnp.where(lane == x.shape[1] - 1, 0.0, pltpu.roll(x, x.shape[1] - 1, 1))


def body(
    side, own, share, height, width,
    img, ker, cot,
    act_out, grad_out, kg_out,
    xs, gs, ss, s3, acc, wk, wpk, wraw, em, wf, wb, ab, pf, pb,
    arrived, kin, kp, kr, ksum, kr2, kt, kq,
    local, wsend, wrecv, isend, irecv, hsend, hrecv, bsend, brecv,
    ssend, srecv, asend, arecv, alocal, plocal, psend, precv, csend, crecv, ksend, krecv,
    fsend, frecv, near_ready, plane_ready, slab_ready,
):
    rows = height // 2
    chunks = rows // ROWS
    chip = 2 * own
    every = 4 * own
    pad_share = wpk.shape[0]
    lanes = s3.shape[1] // 2

    dp = lax.axis_index("dp")
    chan = lax.axis_index("chan")
    row = lax.axis_index("row")
    l = chan // 2
    c = lax.rem(chan, 2)
    sib = 2 * l + 1 - c
    other = 2 * (1 - l)
    y = dp // side
    x = lax.rem(dp, side)
    first = jnp.where(c == 0, x, y)
    second = jnp.where(c == 0, y, x)
    step_first = jnp.where(c == 0, 1, side)
    step_second = jnp.where(c == 0, side, 1)

    def on_first(k):
        f = lax.rem(first + k, side)
        return f, f * step_first + second * step_second

    def on_second(k):
        s = lax.rem(second + k, side)
        return s, first * step_first + s * step_second

    barrier = pltpu.get_barrier_semaphore()

    def tell(sem, **where):
        pl.semaphore_signal(sem, inc=1, device_id=where, device_id_type=MESH)

    tell(barrier, chan=other + 1)

    @pl.when(c == 0)
    def _():
        tell(barrier, chan=sib)

    for k in range(1, side):
        for to in (on_first(k)[1], on_second(k)[1]):
            tell(barrier, dp=to, chan=0)
    tell(barrier, row=1 - row, chan=2)

    def agree(teller, number, sem):
        @pl.when(chan == teller)
        def _():
            pl.semaphore_wait(barrier, number)
            for k in range(1, 4):
                tell(sem, chan=(teller + k) % 4)

        @pl.when(chan != teller)
        def _():
            pl.semaphore_wait(sem, 1)

    def mine(ref, first_row, n, g):
        return ref.at[pl.ds(first_row, n), pl.ds(pl.multiple_of(own * g, 16), own)]

    load_k = pltpu.make_async_copy(ker, wk, local.at[0])
    load_k.start()
    load_x = pltpu.make_async_copy(
        img.at[pl.ds((rows - 1) * c, rows + 1)], mine(xs, 1 - c, rows + 1, chan), local.at[1]
    )
    load_x.start()
    load_g = pltpu.make_async_copy(cot.at[pl.ds(rows * c, rows)], mine(gs, 0, rows, c), local.at[2])
    load_g.start()

    @pl.when(c == 1)
    def _():
        pl.semaphore_wait(barrier, 3)
        tell(near_ready, chan=sib)

    @pl.when(c == 0)
    def _():
        pl.semaphore_wait(near_ready, 1)

    pieces = [(rows - ROWS, ROWS + 1), (1, ROWS + 1)]
    pieces += [(ROWS * k + 2, ROWS) for k in range(1, chunks - 2)]
    pieces += [(ROWS * (chunks - 2) + 2, ROWS - 2)]
    sent = []

    def send(*args, **where):
        copy = remote(*args, **where)
        copy.start()
        sent.append(copy)

    def send_piece(to, s):
        start, n = pieces[s]
        send(
            img.at[pl.ds(rows * to + start - 1, n)], mine(xs, start, n, chan),
            isend.at[to, s], irecv.at[c, s], chan=other + to,
        )

    send_piece(0, 0)
    send_piece(1, 1)
    send(
        img.at[pl.ds((rows - 1) * (1 - c), rows + 1)], mine(xs, c, rows + 1, chan),
        bsend.at[0], brecv.at[0], chan=sib,
    )
    send(cot.at[pl.ds(rows * (1 - c), rows)], mine(gs, 0, rows, c), bsend.at[1], brecv.at[1], chan=sib)
    send_piece(0, 1)
    send_piece(1, 0)
    for to in range(2):
        send_piece(to, 2)

    wpk[...] = jnp.zeros_like(wpk)
    load_k.wait()
    for b in range(3):
        for a in range(3):
            wpk[a * share : (a + 1) * share, b * own : (b + 1) * own] = wk[3 * a + b].astype(F32)
    wraw[c, second, first] = wpk[...].astype(BF16)

    agree(0, 8 * (side - 1), plane_ready)

    gather = []
    for k in range(1, side):
        spot = wraw.at[c, second, first]
        copy = remote(spot, spot, wsend.at[0, k], wrecv.at[0, k], dp=on_first(k)[1])
        copy.start()
        gather.append(copy)

    for core in range(2):
        s3[:, core * lanes + 3 * own : (core + 1) * lanes, :] = jnp.zeros((chunks, lanes - 3 * own, s3.shape[2]), BF16)

    @pl.when(jnp.logical_and(c == 0, row == 0))
    def _():
        xs[0] = jnp.zeros(xs.shape[1:], BF16)
        ss[0] = jnp.zeros(ss.shape[1:], BF16)

    @pl.when(jnp.logical_and(c == 1, row == 1))
    def _():
        xs[rows + 1] = jnp.zeros(xs.shape[1:], BF16)
        ss[rows + 1] = jnp.zeros(ss.shape[1:], BF16)

    acc[...] = jnp.zeros_like(acc)
    spot = lax.broadcasted_iota(jnp.int32, (1, em.shape[1]), 1)
    owner = jnp.zeros_like(spot)
    for k in range(1, side * side):
        owner += (spot >= k * pad_share).astype(jnp.int32)
    within = spot - owner * pad_share
    tap = (within >= share).astype(jnp.int32) + (within >= 2 * share).astype(jnp.int32)
    target = tap * every + owner * share + within - tap * share
    target = jnp.where(within < 3 * share, target, -1)
    em[...] = (lax.broadcasted_iota(jnp.int32, em.shape, 0) == target).astype(F32).astype(BF16)

    agree(2, 4, slab_ready)
    for to in range(2):
        send(
            img.at[pl.ds((height - 1) * (1 - row), 1)], mine(xs, (rows + 1) * row, 1, chan),
            hsend.at[to], hrecv.at[chan], row=1 - row, chan=2 * to + row,
        )
    for s in range(3, chunks):
        for to in range(2):
            send_piece(to, s)

    for copy in gather:
        copy.wait()
    spot = wraw.at[c, second]
    gather = [remote(spot, spot, wsend.at[1, k], wrecv.at[1, k], dp=on_second(k)[1]) for k in range(1, side)]
    for copy in gather:
        copy.start()
    send(spot, spot, fsend.at[0], frecv.at[0], chan=sib)
    for k in range(1, side):
        gather[k - 1].wait()
        spot = wraw.at[c, lax.rem(second + side - k, side)]
        send(spot, spot, fsend.at[k], frecv.at[k], chan=sib)
    for k in range(side):
        spot = wraw.at[1 - c, k]
        remote(spot, spot, fsend.at[k], frecv.at[k], chan=sib).wait_recv()

    for core in range(2):
        order = [(i, j) if core == 0 else (j, i) for i in range(side) for j in range(side)]
        blocks = jnp.concatenate([wraw[core, i, j] for i, j in order], axis=0)
        taps = jnp.dot(em[...], blocks, preferred_element_type=F32)
        turned = jnp.transpose(taps).astype(BF16)
        for b in range(3):
            wf[b * chip + core * own : b * chip + (core + 1) * own, :] = turned[b * own : (b + 1) * own]
        narrow = taps.astype(BF16)
        for a in range(3):
            for b in range(3):
                goal = (2 - a) * chip + core * own
                for part in range(2):
                    base = pl.multiple_of(b * every + chip * jnp.where(l == part, 0, 1), 16)
                    start = a * every + part * chip
                    wb[pl.ds(base, chip), goal : goal + own] = narrow[
                        start : start + chip, b * own : (b + 1) * own
                    ]

    load_x.wait()
    load_g.wait()
    for which, ref in ((0, mine(xs, 1 - c, rows + 1, sib)), (1, mine(gs, 0, rows, 1 - c))):
        remote(ref, ref, bsend.at[which], brecv.at[which], chan=sib).wait_recv()
    def border():
        at = pl.ds(pl.multiple_of(own * other, 16), chip)
        return remote(
            xs.at[jnp.where(c == 0, rows, 1), at], xs.at[jnp.where(c == 0, 0, rows + 1), at],
            bsend.at[3], brecv.at[3], chan=sib,
        )

    def await_rows(s, start, n):
        for of in range(2):
            ref = mine(xs, start, n, other + of)
            remote(ref, ref, isend.at[of, s], irecv.at[of, s], chan=other + of).wait_recv()

    place = 2 * row + c

    def down_copy():
        return remote(ss.at[rows], ss.at[0], ssend.at[0], srecv.at[0], row=row + c, chan=sib)

    def up_copy():
        return remote(ss.at[1], ss.at[rows + 1], ssend.at[1], srecv.at[1], row=row - (1 - c), chan=sib)

    def trade():
        return remote(acc.at[1 - c], kin, ksend.at[0, 0], krecv.at[0, 0], chan=sib)

    def plane_copies():
        made = []
        for k in range(1, side):
            f, to = on_first(k)
            made.append(remote(kp.at[f], kr.at[k], ksend.at[1, k], krecv.at[1, k], dp=to))
        return made

    def act_copies(k):
        at = pl.ds(k * ROWS, ROWS)
        to = pl.ds(rows * c + k * ROWS, ROWS)
        return (
            pltpu.make_async_copy(ab.at[c, at], act_out.at[to], alocal.at[k]),
            remote(ab.at[1 - c, at], act_out.at[to], asend.at[k], arecv.at[k], chan=sib),
        )

    def near_copies(k):
        at = pl.ds(k * ROWS, ROWS)
        to = pl.ds(rows * c + k * ROWS, ROWS)
        return (
            pltpu.make_async_copy(pf.at[c, at], grad_out.at[to], plocal.at[k]),
            remote(pf.at[1 - c, at], grad_out.at[to], psend.at[k], precv.at[k], chan=sib),
        )

    def far_copies(k):
        at = pl.ds(k * ROWS, ROWS)
        to = pl.ds(rows * c + k * ROWS, ROWS)
        return (
            remote(pb.at[0, at], arrived.at[to], csend.at[0, k], crecv.at[c, k], chan=other),
            remote(pb.at[1, at], arrived.at[to], csend.at[1, k], crecv.at[c, k], chan=other + 1),
        )

    def chunk_at(s):
        return jnp.where(s < 2, jnp.where(s == c, chunks - 1, 0), s - 1)

    def three(ref, start):
        block = ref[pl.ds(start, 3)]
        return block.reshape(3 * ref.shape[1], width)

    def forward(k):
        for pair in range(ROWS // 2):
            q = k * ROWS + 2 * pair
            right = jnp.concatenate([three(xs, q), three(xs, q + 1)], axis=1)
            taps = jnp.dot(wf[...], right, preferred_element_type=F32)
            for u in range(2):
                at = slice(u * width, (u + 1) * width)
                pre = shift_right(taps[0:chip, at]) + taps[chip : 2 * chip, at] + shift_left(taps[2 * chip :, at])
                sigma = 1.0 / (1.0 + jnp.exp(-pre))
                done = (pre * sigma).astype(BF16)
                for core in range(2):
                    ab[core, q + u] = done[core * own : (core + 1) * own]
                slope = gs[q + u].astype(F32) * sigma * (1.0 + pre * (1.0 - sigma))
                slope = slope.astype(BF16)
                ss[q + u + 1] = slope
                wide_slope = slope.astype(F32)
                turned = (shift_left(wide_slope).astype(BF16), slope, shift_right(wide_slope).astype(BF16))
                to = slice((2 * pair + u) * width, (2 * pair + u + 1) * width)
                for core in range(2):
                    for b in range(3):
                        s3[k, core * lanes + b * own : core * lanes + (b + 1) * own, to] = turned[b][
                            core * own : (core + 1) * own
                        ]

    def kernel_terms(k):
        left = jnp.concatenate([three(xs, k * ROWS + u) for u in range(ROWS)], axis=1)
        term = lax.dot_general(left, s3[k], (((1,), (1,)), ((), ())), preferred_element_type=F32)
        for core in range(2):
            acc[core] += term[:, core * lanes : (core + 1) * lanes]

    def backward(k):
        for pair in range(ROWS // 2):
            q = k * ROWS + 2 * pair
            right = jnp.concatenate([three(ss, q), three(ss, q + 1)], axis=1)
            taps = jnp.dot(wb[...], right, preferred_element_type=F32)
            for u in range(2):
                at = slice(u * width, (u + 1) * width)
                grad = (
                    shift_left(taps[0:every, at])
                    + taps[every : 2 * every, at]
                    + shift_right(taps[2 * every :, at])
                )
                for core in range(2):
                    pf[core, q + u] = grad[core * own : (core + 1) * own]
                    pb[core, q + u] = grad[chip + core * own : chip + (core + 1) * own].astype(BF16)

    steps = chunks + LAG

    @pl.loop(0, steps)
    def _(s):
        @pl.when(s < 2)
        def _():
            piece = jnp.where(s == 0, c, 1 - c)
            await_rows(piece, jnp.where(piece == 0, rows - ROWS, 1), ROWS + 1)

        @pl.when(s == 0)
        def _():
            border().start()
            border().wait_recv()

        @pl.when(jnp.logical_and(s == 1, c != row))
        def _():
            for g in range(4):
                ref = mine(xs, (rows + 1) * c, 1, g)
                remote(ref, ref, hsend.at[0], hrecv.at[g], row=1 - row, chan=g).wait_recv()

        @pl.when(s == chunks - 1)
        def _():
            await_rows(chunks - 1, *pieces[chunks - 1])

        @pl.when(jnp.logical_and(s > 1, s < chunks - 1))
        def _():
            await_rows(s, ROWS * (s - 1) + 2, ROWS)

        @pl.when(s < chunks)
        def _():
            k = chunk_at(s)
            forward(k)
            for copy in act_copies(k):
                copy.start()

        @pl.when(jnp.logical_and(s >= chunks // 2, s < chunks))
        def _():
            kernel_terms(chunk_at(2 * s - chunks + 1))

        @pl.when(jnp.logical_and(s >= chunks // 2 - 1, s < chunks - 1))
        def _():
            kernel_terms(chunk_at(2 * s - chunks + 2))

        @pl.when(jnp.logical_and(s == c, place < 3))
        def _():
            down_copy().start()

        @pl.when(jnp.logical_and(s == 1 - c, place > 0))
        def _():
            up_copy().start()

        @pl.when(s == chunks - 1)
        def _():
            trade().start()

        @pl.when(jnp.logical_and(s == steps - 2, place < 3))
        def _():
            up_copy().wait_recv()

        @pl.when(jnp.logical_and(s == steps - 1, place > 0))
        def _():
            down_copy().wait_recv()

        @pl.when(s >= LAG)
        def _():
            k = lax.rem(s - LAG + 1, chunks)
            backward(k)
            for copy in near_copies(k):
                copy.start()

            @pl.when(s < steps - HELD)
            def _():
                for copy in far_copies(k):
                    copy.start()

        @pl.when(s == chunks - 1)
        def _():
            trade().wait()
            kin[...] += acc[c]
            for i in range(side):
                for j in range(side):
                    f = jnp.where(c == 0, j, i)
                    to = jnp.where(c == 0, i, j)
                    d = i * side + j
                    for a in range(3):
                        kp[f, to, a * share : (a + 1) * share, :] = kin[
                            a * every + d * share : a * every + (d + 1) * share, :
                        ]
            for copy in plane_copies():
                copy.start()

    for copy in plane_copies():
        copy.wait()
    total = kp[first]
    for k in range(1, side):
        total += kr[k]
    ksum[...] = total
    copies = []
    for k in range(1, side):
        s, to = on_second(k)
        copy = remote(ksum.at[s], kr2.at[k], ksend.at[2, k], krecv.at[2, k], dp=to)
        copy.start()
        copies.append(copy)
    for copy in copies:
        copy.wait()
    total = ksum[second]
    for k in range(1, side):
        total += kr2[k]
    kt[...] = total.astype(BF16)
    copy = remote(kt, kq, ksend.at[3, 0], krecv.at[3, 0], row=1 - row)
    copy.start()
    for s in range(steps - HELD, steps):
        for far in far_copies((s - LAG + 1) % chunks):
            far.start()

    for old in sent:
        old.wait_send()
    border().wait_send()

    @pl.when(place < 3)
    def _():
        down_copy().wait_send()

    @pl.when(place > 0)
    def _():
        up_copy().wait_send()

    @pl.loop(0, chunks)
    def _(k):
        for old in act_copies(k):
            old.wait()


    @pl.loop(1, chunks + 1)
    def _(k):
        k = lax.rem(k, chunks)
        for old in near_copies(k):
            old.wait()
        for of in range(2):
            at = pl.ds(rows * of + k * ROWS, ROWS)
            ref = arrived.at[at]
            remote(ref, ref, csend.at[of, k], crecv.at[of, k], chan=other + of).wait_recv()
            grad_out[at] += arrived[at].astype(F32)
        for old in far_copies(k):
            old.wait_send()

    copy.wait()
    kg_out[...] = kt[...].astype(F32) + kq[...].astype(F32)


def finish(own, share, act, grad, terms, act_out, grad_out, kg_out, kg, sems):
    step = grad.shape[0] // PARTS
    copies = []
    for p in range(PARTS):
        at = pl.ds(p * step, step)
        copies.append(pltpu.make_async_copy(grad.at[at], grad_out.at[at], sems.at[p, 0]))
        copies.append(pltpu.make_async_copy(act.at[at], act_out.at[at], sems.at[p, 1]))
    for copy in copies:
        copy.start()
    for a in range(3):
        for b in range(3):
            kg[3 * a + b] = terms[a * share : (a + 1) * share, b * own : (b + 1) * own]
    last = pltpu.make_async_copy(kg, kg_out, sems.at[PARTS, 0])
    last.start()
    for copy in copies:
        copy.wait()
    last.wait()


def shards(images, kernel, cotangent):
    _, height, own, width = images.shape
    share = kernel.shape[1]
    side = math.isqrt(lax.axis_size("dp"))
    rows = height // 2
    chunks = rows // ROWS
    chip, every = 2 * own, 4 * own
    pad_share = round_up(3 * share, 16)
    lanes = round_up(3 * own, 128)
    dma = pltpu.SemaphoreType.DMA
    scratch = [
        pltpu.VMEM((rows + 2, every, width), BF16),
        pltpu.VMEM((rows, chip, width), BF16),
        pltpu.VMEM((rows + 2, chip, width), BF16),
        pltpu.VMEM((chunks, 2 * lanes, ROWS * width), BF16),
        pltpu.VMEM((2, 3 * every, lanes), F32),
        pltpu.VMEM(kernel.shape, BF16),
        pltpu.VMEM((pad_share, lanes), F32),
        pltpu.VMEM((2, side, side, pad_share, lanes), BF16),
        pltpu.VMEM((3 * every, side * side * pad_share), BF16),
        pltpu.VMEM((3 * chip, 3 * every), BF16),
        pltpu.VMEM((3 * every, 3 * chip), BF16),
        pltpu.VMEM((2, rows, own, width), BF16),
        pltpu.VMEM((2, rows, own, width), F32),
        pltpu.VMEM((2, rows, own, width), BF16),
        pltpu.VMEM((height, own, width), BF16),
        pltpu.VMEM((3 * every, lanes), F32),
        pltpu.VMEM((side, side, pad_share, lanes), F32),
        pltpu.VMEM((side, side, pad_share, lanes), F32),
        pltpu.VMEM((side, pad_share, lanes), F32),
        pltpu.VMEM((side, pad_share, lanes), F32),
        pltpu.VMEM((pad_share, lanes), BF16),
        pltpu.VMEM((pad_share, lanes), BF16),
        dma((3,)),
        dma((2, side)), dma((2, side)),
        dma((2, chunks)), dma((2, chunks)),
        dma((2,)), dma((4,)),
        dma((4,)), dma((4,)),
        dma((2,)), dma((2,)),
        dma((chunks,)), dma((chunks,)), dma((chunks,)),
        dma((chunks,)), dma((chunks,)), dma((chunks,)),
        dma((2, chunks)), dma((2, chunks)),
        dma((4, side)), dma((4, side)),
        dma((side,)), dma((side,)),
        pltpu.SemaphoreType.REGULAR, pltpu.SemaphoreType.REGULAR, pltpu.SemaphoreType.REGULAR,
    ]
    hbm = pl.BlockSpec(memory_space=pl.ANY)
    vmem = pl.BlockSpec(memory_space=pltpu.VMEM)
    activated, input_grad, terms = pl.pallas_call(
        functools.partial(body, side, own, share, height, width),
        out_shape=(
            pltpu.VMEM((height, own, width), BF16),
            pltpu.VMEM((height, own, width), F32),
            pltpu.VMEM((pad_share, lanes), F32),
        ),
        in_specs=[hbm] * 3,
        out_specs=(vmem,) * 3,
        scratch_shapes=scratch,
        compiler_params=pltpu.CompilerParams(
            collective_id=0, has_side_effects=True, vmem_limit_bytes=56 * 2**20
        ),
        name="conv_block",
    )(images[0], kernel, cotangent[0])
    activated, input_grad, kernel_grad = pl.pallas_call(
        functools.partial(finish, own, share),
        out_shape=(
            jax.ShapeDtypeStruct((height, own, width), BF16),
            jax.ShapeDtypeStruct((height, own, width), F32),
            jax.ShapeDtypeStruct((9, share, own), F32),
        ),
        in_specs=[vmem] * 3,
        out_specs=(hbm, hbm, hbm),
        scratch_shapes=[pltpu.VMEM((9, share, own), F32), dma((PARTS + 1, 2))],
        compiler_params=pltpu.CompilerParams(vmem_limit_bytes=16 * 2**20),
        name="results",
    )(activated, input_grad, terms)
    return activated[None], input_grad[None], kernel_grad


def solution(mesh):
    placed = (P("dp", "row", "chan", None), P(None, "dp", "chan"), P("dp", "row", "chan", None))
    return jax.shard_map(
        shards,
        mesh=mesh,
        in_specs=placed,
        out_specs=(
            P("dp", "row", "chan", None),
            P("dp", "row", "chan", None),
            P(None, "dp", "chan"),
        ),
        check_vma=False,
    )
```

```python
import functools
import math

import jax
import jax.numpy as jnp
from jax import lax
from jax.experimental import pallas as pl
from jax.experimental.pallas import tpu as pltpu
from jax.sharding import PartitionSpec as P

MESH = pl.DeviceIdType.MESH
BF16 = jnp.bfloat16
F32 = jnp.float32
ROWS = 4
PARTS = 4
LAG = 3
HELD = 1


def round_up(x, m):
    return (x + m - 1) // m * m


def remote(src, dst, send, recv, **where):
    return pltpu.make_async_remote_copy(
        src_ref=src, dst_ref=dst, send_sem=send, recv_sem=recv, device_id=where, device_id_type=MESH
    )


def shift_right(x):
    lane = lax.broadcasted_iota(jnp.int32, x.shape, 1)
    return jnp.where(lane == 0, 0.0, pltpu.roll(x, 1, 1))


def shift_left(x):
    lane = lax.broadcasted_iota(jnp.int32, x.shape, 1)
    return jnp.where(lane == x.shape[1] - 1, 0.0, pltpu.roll(x, x.shape[1] - 1, 1))


def body(
    side, own, share, height, width,
    img, ker, cot,
    act_out, grad_out, kg_out,
    xs, gs, ss, s3, acc, wk, wpk, wraw, em, wf, wb, ab, pf, pb,
    arrived, kin, kp, kr, ksum, kr2, kt, kq,
    local, wsend, wrecv, isend, irecv, hsend, hrecv, bsend, brecv,
    ssend, srecv, asend, arecv, alocal, plocal, psend, precv, csend, crecv, ksend, krecv,
    fsend, frecv, near_ready, plane_ready, slab_ready,
):
    rows = height // 2
    chunks = rows // ROWS
    chip = 2 * own
    every = 4 * own
    pad_share = wpk.shape[0]
    lanes = s3.shape[1] // 2

    dp = lax.axis_index("dp")
    chan = lax.axis_index("chan")
    row = lax.axis_index("row")
    l = chan // 2
    c = lax.rem(chan, 2)
    sib = 2 * l + 1 - c
    other = 2 * (1 - l)
    y = dp // side
    x = lax.rem(dp, side)
    first = jnp.where(c == 0, x, y)
    second = jnp.where(c == 0, y, x)
    step_first = jnp.where(c == 0, 1, side)
    step_second = jnp.where(c == 0, side, 1)

    def on_first(k):
        f = lax.rem(first + k, side)
        return f, f * step_first + second * step_second

    def on_second(k):
        s = lax.rem(second + k, side)
        return s, first * step_first + s * step_second

    barrier = pltpu.get_barrier_semaphore()

    def tell(sem, **where):
        pl.semaphore_signal(sem, inc=1, device_id=where, device_id_type=MESH)

    tell(barrier, chan=other + 1)

    @pl.when(c == 0)
    def _():
        tell(barrier, chan=sib)

    for k in range(1, side):
        for to in (on_first(k)[1], on_second(k)[1]):
            tell(barrier, dp=to, chan=0)
    tell(barrier, row=1 - row, chan=2)

    def agree(teller, number, sem):
        @pl.when(chan == teller)
        def _():
            pl.semaphore_wait(barrier, number)
            for k in range(1, 4):
                tell(sem, chan=(teller + k) % 4)

        @pl.when(chan != teller)
        def _():
            pl.semaphore_wait(sem, 1)

    def mine(ref, first_row, n, g):
        return ref.at[pl.ds(first_row, n), pl.ds(pl.multiple_of(own * g, 16), own)]

    load_k = pltpu.make_async_copy(ker, wk, local.at[0])
    load_k.start()
    load_x = pltpu.make_async_copy(
        img.at[pl.ds((rows - 1) * c, rows + 1)], mine(xs, 1 - c, rows + 1, chan), local.at[1]
    )
    load_x.start()
    load_g = pltpu.make_async_copy(cot.at[pl.ds(rows * c, rows)], mine(gs, 0, rows, c), local.at[2])
    load_g.start()

    @pl.when(c == 1)
    def _():
        pl.semaphore_wait(barrier, 3)
        tell(near_ready, chan=sib)

    @pl.when(c == 0)
    def _():
        pl.semaphore_wait(near_ready, 1)

    pieces = [(rows - ROWS, ROWS + 1), (1, ROWS + 1)]
    pieces += [(ROWS * k + 2, ROWS) for k in range(1, chunks - 2)]
    pieces += [(ROWS * (chunks - 2) + 2, ROWS - 2)]
    sent = []

    def send(*args, **where):
        copy = remote(*args, **where)
        copy.start()
        sent.append(copy)

    def send_piece(to, s):
        start, n = pieces[s]
        send(
            img.at[pl.ds(rows * to + start - 1, n)], mine(xs, start, n, chan),
            isend.at[to, s], irecv.at[c, s], chan=other + to,
        )

    send_piece(0, 0)
    send_piece(1, 1)
    send(
        img.at[pl.ds((rows - 1) * (1 - c), rows + 1)], mine(xs, c, rows + 1, chan),
        bsend.at[0], brecv.at[0], chan=sib,
    )
    send(cot.at[pl.ds(rows * (1 - c), rows)], mine(gs, 0, rows, c), bsend.at[1], brecv.at[1], chan=sib)
    send_piece(0, 1)
    send_piece(1, 0)
    wpk[...] = jnp.zeros_like(wpk)
    load_k.wait()
    for b in range(3):
        for a in range(3):
            wpk[a * share : (a + 1) * share, b * own : (b + 1) * own] = wk[3 * a + b].astype(F32)
    wraw[c, second, first] = wpk[...].astype(BF16)

    agree(0, 8 * (side - 1), plane_ready)

    gather = []
    for k in range(1, side):
        spot = wraw.at[c, second, first]
        copy = remote(spot, spot, wsend.at[0, k], wrecv.at[0, k], dp=on_first(k)[1])
        copy.start()
        gather.append(copy)

    for core in range(2):
        s3[:, core * lanes + 3 * own : (core + 1) * lanes, :] = jnp.zeros((chunks, lanes - 3 * own, s3.shape[2]), BF16)

    @pl.when(jnp.logical_and(c == 0, row == 0))
    def _():
        xs[0] = jnp.zeros(xs.shape[1:], BF16)
        ss[0] = jnp.zeros(ss.shape[1:], BF16)

    @pl.when(jnp.logical_and(c == 1, row == 1))
    def _():
        xs[rows + 1] = jnp.zeros(xs.shape[1:], BF16)
        ss[rows + 1] = jnp.zeros(ss.shape[1:], BF16)

    acc[...] = jnp.zeros_like(acc)
    spot = lax.broadcasted_iota(jnp.int32, (1, em.shape[1]), 1)
    owner = jnp.zeros_like(spot)
    for k in range(1, side * side):
        owner += (spot >= k * pad_share).astype(jnp.int32)
    within = spot - owner * pad_share
    tap = (within >= share).astype(jnp.int32) + (within >= 2 * share).astype(jnp.int32)
    target = tap * every + owner * share + within - tap * share
    target = jnp.where(within < 3 * share, target, -1)
    em[...] = (lax.broadcasted_iota(jnp.int32, em.shape, 0) == target).astype(F32).astype(BF16)

    agree(2, 4, slab_ready)
    for to in range(2):
        send(
            img.at[pl.ds((height - 1) * (1 - row), 1)], mine(xs, (rows + 1) * row, 1, chan),
            hsend.at[to], hrecv.at[chan], row=1 - row, chan=2 * to + row,
        )
    for s in range(2, chunks):
        for to in range(2):
            send_piece(to, s)

    for copy in gather:
        copy.wait()
    spot = wraw.at[c, second]
    gather = [remote(spot, spot, wsend.at[1, k], wrecv.at[1, k], dp=on_second(k)[1]) for k in range(1, side)]
    for copy in gather:
        copy.start()
    send(spot, spot, fsend.at[0], frecv.at[0], chan=sib)
    for k in range(1, side):
        gather[k - 1].wait()
        spot = wraw.at[c, lax.rem(second + side - k, side)]
        send(spot, spot, fsend.at[k], frecv.at[k], chan=sib)
    for k in range(side):
        spot = wraw.at[1 - c, k]
        remote(spot, spot, fsend.at[k], frecv.at[k], chan=sib).wait_recv()

    for core in range(2):
        order = [(i, j) if core == 0 else (j, i) for i in range(side) for j in range(side)]
        blocks = jnp.concatenate([wraw[core, i, j] for i, j in order], axis=0)
        taps = jnp.dot(em[...], blocks, preferred_element_type=F32)
        turned = jnp.transpose(taps).astype(BF16)
        for b in range(3):
            wf[b * chip + core * own : b * chip + (core + 1) * own, :] = turned[b * own : (b + 1) * own]
        narrow = taps.astype(BF16)
        for a in range(3):
            for b in range(3):
                goal = (2 - a) * chip + core * own
                for part in range(2):
                    base = pl.multiple_of(b * every + chip * jnp.where(l == part, 0, 1), 16)
                    start = a * every + part * chip
                    wb[pl.ds(base, chip), goal : goal + own] = narrow[
                        start : start + chip, b * own : (b + 1) * own
                    ]

    load_x.wait()
    load_g.wait()
    for which, ref in ((0, mine(xs, 1 - c, rows + 1, sib)), (1, mine(gs, 0, rows, 1 - c))):
        remote(ref, ref, bsend.at[which], brecv.at[which], chan=sib).wait_recv()
    def border():
        at = pl.ds(pl.multiple_of(own * other, 16), chip)
        return remote(
            xs.at[jnp.where(c == 0, rows, 1), at], xs.at[jnp.where(c == 0, 0, rows + 1), at],
            bsend.at[3], brecv.at[3], chan=sib,
        )

    def await_rows(s, start, n):
        for of in range(2):
            ref = mine(xs, start, n, other + of)
            remote(ref, ref, isend.at[of, s], irecv.at[of, s], chan=other + of).wait_recv()

    place = 2 * row + c

    def down_copy():
        return remote(ss.at[rows], ss.at[0], ssend.at[0], srecv.at[0], row=row + c, chan=sib)

    def up_copy():
        return remote(ss.at[1], ss.at[rows + 1], ssend.at[1], srecv.at[1], row=row - (1 - c), chan=sib)

    def trade():
        return remote(acc.at[1 - c], kin, ksend.at[0, 0], krecv.at[0, 0], chan=sib)

    def plane_copies():
        made = []
        for k in range(1, side):
            f, to = on_first(k)
            made.append(remote(kp.at[f], kr.at[k], ksend.at[1, k], krecv.at[1, k], dp=to))
        return made

    def act_copies(k):
        at = pl.ds(k * ROWS, ROWS)
        to = pl.ds(rows * c + k * ROWS, ROWS)
        return (
            pltpu.make_async_copy(ab.at[c, at], act_out.at[to], alocal.at[k]),
            remote(ab.at[1 - c, at], act_out.at[to], asend.at[k], arecv.at[k], chan=sib),
        )

    def near_copies(k):
        at = pl.ds(k * ROWS, ROWS)
        to = pl.ds(rows * c + k * ROWS, ROWS)
        return (
            pltpu.make_async_copy(pf.at[c, at], grad_out.at[to], plocal.at[k]),
            remote(pf.at[1 - c, at], grad_out.at[to], psend.at[k], precv.at[k], chan=sib),
        )

    def far_copies(k):
        at = pl.ds(k * ROWS, ROWS)
        to = pl.ds(rows * c + k * ROWS, ROWS)
        return (
            remote(pb.at[0, at], arrived.at[to], csend.at[0, k], crecv.at[c, k], chan=other),
            remote(pb.at[1, at], arrived.at[to], csend.at[1, k], crecv.at[c, k], chan=other + 1),
        )

    def chunk_at(s):
        return jnp.where(s < 2, jnp.where(s == c, chunks - 1, 0), s - 1)

    def three(ref, start):
        block = ref[pl.ds(start, 3)]
        return block.reshape(3 * ref.shape[1], width)

    def forward(k):
        for pair in range(ROWS // 2):
            q = k * ROWS + 2 * pair
            right = jnp.concatenate([three(xs, q), three(xs, q + 1)], axis=1)
            taps = jnp.dot(wf[...], right, preferred_element_type=F32)
            for u in range(2):
                at = slice(u * width, (u + 1) * width)
                pre = shift_right(taps[0:chip, at]) + taps[chip : 2 * chip, at] + shift_left(taps[2 * chip :, at])
                sigma = 1.0 / (1.0 + jnp.exp(-pre))
                done = (pre * sigma).astype(BF16)
                for core in range(2):
                    ab[core, q + u] = done[core * own : (core + 1) * own]
                slope = gs[q + u].astype(F32) * sigma * (1.0 + pre * (1.0 - sigma))
                slope = slope.astype(BF16)
                ss[q + u + 1] = slope
                wide_slope = slope.astype(F32)
                turned = (shift_left(wide_slope).astype(BF16), slope, shift_right(wide_slope).astype(BF16))
                to = slice((2 * pair + u) * width, (2 * pair + u + 1) * width)
                for core in range(2):
                    for b in range(3):
                        s3[k, core * lanes + b * own : core * lanes + (b + 1) * own, to] = turned[b][
                            core * own : (core + 1) * own
                        ]

    def kernel_terms(k):
        left = jnp.concatenate([three(xs, k * ROWS + u) for u in range(ROWS)], axis=1)
        term = lax.dot_general(left, s3[k], (((1,), (1,)), ((), ())), preferred_element_type=F32)
        for core in range(2):
            acc[core] += term[:, core * lanes : (core + 1) * lanes]

    def backward(k):
        for pair in range(ROWS // 2):
            q = k * ROWS + 2 * pair
            right = jnp.concatenate([three(ss, q), three(ss, q + 1)], axis=1)
            taps = jnp.dot(wb[...], right, preferred_element_type=F32)
            for u in range(2):
                at = slice(u * width, (u + 1) * width)
                grad = (
                    shift_left(taps[0:every, at])
                    + taps[every : 2 * every, at]
                    + shift_right(taps[2 * every :, at])
                )
                for core in range(2):
                    pf[core, q + u] = grad[core * own : (core + 1) * own]
                    pb[core, q + u] = grad[chip + core * own : chip + (core + 1) * own].astype(BF16)

    steps = chunks + LAG

    @pl.loop(0, steps)
    def _(s):
        @pl.when(s < 2)
        def _():
            piece = jnp.where(s == 0, c, 1 - c)
            await_rows(piece, jnp.where(piece == 0, rows - ROWS, 1), ROWS + 1)

        @pl.when(s == 0)
        def _():
            border().start()
            border().wait_recv()

        @pl.when(jnp.logical_and(s == 1, c != row))
        def _():
            for g in range(4):
                ref = mine(xs, (rows + 1) * c, 1, g)
                remote(ref, ref, hsend.at[0], hrecv.at[g], row=1 - row, chan=g).wait_recv()

        @pl.when(s == chunks - 1)
        def _():
            await_rows(chunks - 1, *pieces[chunks - 1])

        @pl.when(jnp.logical_and(s > 1, s < chunks - 1))
        def _():
            await_rows(s, ROWS * (s - 1) + 2, ROWS)

        @pl.when(s < chunks)
        def _():
            k = chunk_at(s)
            forward(k)
            for copy in act_copies(k):
                copy.start()

        @pl.when(jnp.logical_and(s >= chunks // 2, s < chunks))
        def _():
            kernel_terms(chunk_at(2 * s - chunks + 1))

        @pl.when(jnp.logical_and(s >= chunks // 2 - 1, s < chunks - 1))
        def _():
            kernel_terms(chunk_at(2 * s - chunks + 2))

        @pl.when(jnp.logical_and(s == c, place < 3))
        def _():
            down_copy().start()

        @pl.when(jnp.logical_and(s == 1 - c, place > 0))
        def _():
            up_copy().start()

        @pl.when(s == chunks - 1)
        def _():
            trade().start()

        @pl.when(jnp.logical_and(s == steps - 2, place < 3))
        def _():
            up_copy().wait_recv()

        @pl.when(jnp.logical_and(s == steps - 1, place > 0))
        def _():
            down_copy().wait_recv()

        @pl.when(s >= LAG)
        def _():
            k = lax.rem(s - LAG + 1, chunks)
            backward(k)
            for copy in near_copies(k):
                copy.start()

            @pl.when(s < steps - HELD)
            def _():
                for copy in far_copies(k):
                    copy.start()

        @pl.when(s == chunks - 1)
        def _():
            trade().wait()
            kin[...] += acc[c]
            for i in range(side):
                for j in range(side):
                    f = jnp.where(c == 0, j, i)
                    to = jnp.where(c == 0, i, j)
                    d = i * side + j
                    for a in range(3):
                        kp[f, to, a * share : (a + 1) * share, :] = kin[
                            a * every + d * share : a * every + (d + 1) * share, :
                        ]
            for copy in plane_copies():
                copy.start()

    for copy in plane_copies():
        copy.wait()
    total = kp[first]
    for k in range(1, side):
        total += kr[k]
    ksum[...] = total
    copies = []
    for k in range(1, side):
        s, to = on_second(k)
        copy = remote(ksum.at[s], kr2.at[k], ksend.at[2, k], krecv.at[2, k], dp=to)
        copy.start()
        copies.append(copy)
    for copy in copies:
        copy.wait()
    total = ksum[second]
    for k in range(1, side):
        total += kr2[k]
    kt[...] = total.astype(BF16)
    copy = remote(kt, kq, ksend.at[3, 0], krecv.at[3, 0], row=1 - row)
    copy.start()
    for s in range(steps - HELD, steps):
        for far in far_copies((s - LAG + 1) % chunks):
            far.start()

    for old in sent:
        old.wait_send()
    border().wait_send()

    @pl.when(place < 3)
    def _():
        down_copy().wait_send()

    @pl.when(place > 0)
    def _():
        up_copy().wait_send()

    @pl.loop(0, chunks)
    def _(k):
        for old in act_copies(k):
            old.wait()


    @pl.loop(1, chunks + 1)
    def _(k):
        k = lax.rem(k, chunks)
        for old in near_copies(k):
            old.wait()
        for of in range(2):
            at = pl.ds(rows * of + k * ROWS, ROWS)
            ref = arrived.at[at]
            remote(ref, ref, csend.at[of, k], crecv.at[of, k], chan=other + of).wait_recv()
            grad_out[at] += arrived[at].astype(F32)
        for old in far_copies(k):
            old.wait_send()

    copy.wait()
    kg_out[...] = kt[...].astype(F32) + kq[...].astype(F32)


def finish(own, share, act, grad, terms, act_out, grad_out, kg_out, kg, sems):
    step = grad.shape[0] // PARTS
    copies = []
    for p in range(PARTS):
        at = pl.ds(p * step, step)
        copies.append(pltpu.make_async_copy(grad.at[at], grad_out.at[at], sems.at[p, 0]))
        copies.append(pltpu.make_async_copy(act.at[at], act_out.at[at], sems.at[p, 1]))
    for copy in copies:
        copy.start()
    for a in range(3):
        for b in range(3):
            kg[3 * a + b] = terms[a * share : (a + 1) * share, b * own : (b + 1) * own]
    last = pltpu.make_async_copy(kg, kg_out, sems.at[PARTS, 0])
    last.start()
    for copy in copies:
        copy.wait()
    last.wait()


def shards(images, kernel, cotangent):
    _, height, own, width = images.shape
    share = kernel.shape[1]
    side = math.isqrt(lax.axis_size("dp"))
    rows = height // 2
    chunks = rows // ROWS
    chip, every = 2 * own, 4 * own
    pad_share = round_up(3 * share, 16)
    lanes = round_up(3 * own, 128)
    dma = pltpu.SemaphoreType.DMA
    scratch = [
        pltpu.VMEM((rows + 2, every, width), BF16),
        pltpu.VMEM((rows, chip, width), BF16),
        pltpu.VMEM((rows + 2, chip, width), BF16),
        pltpu.VMEM((chunks, 2 * lanes, ROWS * width), BF16),
        pltpu.VMEM((2, 3 * every, lanes), F32),
        pltpu.VMEM(kernel.shape, BF16),
        pltpu.VMEM((pad_share, lanes), F32),
        pltpu.VMEM((2, side, side, pad_share, lanes), BF16),
        pltpu.VMEM((3 * every, side * side * pad_share), BF16),
        pltpu.VMEM((3 * chip, 3 * every), BF16),
        pltpu.VMEM((3 * every, 3 * chip), BF16),
        pltpu.VMEM((2, rows, own, width), BF16),
        pltpu.VMEM((2, rows, own, width), F32),
        pltpu.VMEM((2, rows, own, width), BF16),
        pltpu.VMEM((height, own, width), BF16),
        pltpu.VMEM((3 * every, lanes), F32),
        pltpu.VMEM((side, side, pad_share, lanes), F32),
        pltpu.VMEM((side, side, pad_share, lanes), F32),
        pltpu.VMEM((side, pad_share, lanes), F32),
        pltpu.VMEM((side, pad_share, lanes), F32),
        pltpu.VMEM((pad_share, lanes), BF16),
        pltpu.VMEM((pad_share, lanes), BF16),
        dma((3,)),
        dma((2, side)), dma((2, side)),
        dma((2, chunks)), dma((2, chunks)),
        dma((2,)), dma((4,)),
        dma((4,)), dma((4,)),
        dma((2,)), dma((2,)),
        dma((chunks,)), dma((chunks,)), dma((chunks,)),
        dma((chunks,)), dma((chunks,)), dma((chunks,)),
        dma((2, chunks)), dma((2, chunks)),
        dma((4, side)), dma((4, side)),
        dma((side,)), dma((side,)),
        pltpu.SemaphoreType.REGULAR, pltpu.SemaphoreType.REGULAR, pltpu.SemaphoreType.REGULAR,
    ]
    hbm = pl.BlockSpec(memory_space=pl.ANY)
    vmem = pl.BlockSpec(memory_space=pltpu.VMEM)
    activated, input_grad, terms = pl.pallas_call(
        functools.partial(body, side, own, share, height, width),
        out_shape=(
            pltpu.VMEM((height, own, width), BF16),
            pltpu.VMEM((height, own, width), F32),
            pltpu.VMEM((pad_share, lanes), F32),
        ),
        in_specs=[hbm] * 3,
        out_specs=(vmem,) * 3,
        scratch_shapes=scratch,
        compiler_params=pltpu.CompilerParams(
            collective_id=0, has_side_effects=True, vmem_limit_bytes=56 * 2**20
        ),
        name="conv_block",
    )(images[0], kernel, cotangent[0])
    activated, input_grad, kernel_grad = pl.pallas_call(
        functools.partial(finish, own, share),
        out_shape=(
            jax.ShapeDtypeStruct((height, own, width), BF16),
            jax.ShapeDtypeStruct((height, own, width), F32),
            jax.ShapeDtypeStruct((9, share, own), F32),
        ),
        in_specs=[vmem] * 3,
        out_specs=(hbm, hbm, hbm),
        scratch_shapes=[pltpu.VMEM((9, share, own), F32), dma((PARTS + 1, 2))],
        compiler_params=pltpu.CompilerParams(vmem_limit_bytes=16 * 2**20),
        name="results",
    )(activated, input_grad, terms)
    return activated[None], input_grad[None], kernel_grad


def solution(mesh):
    placed = (P("dp", "row", "chan", None), P(None, "dp", "chan"), P("dp", "row", "chan", None))
    return jax.shard_map(
        shards,
        mesh=mesh,
        in_specs=placed,
        out_specs=(
            P("dp", "row", "chan", None),
            P("dp", "row", "chan", None),
            P(None, "dp", "chan"),
        ),
        check_vma=False,
    )
```
